256 devices in a mesh: expert: 32 (over x, z), replica: 4 (over y), tensor: 2 (over core).
Axes of the slice: x: 4, y: 4, z: 8, core: 2. Of those that a mesh axis runs over, the one named last changes fastest.
Arguments:
- grad_out: bfloat16 [16384, 3584], P(('expert', 'replica')), may hold values from -6 to 6
- gates: float32 [16384, 4], P(('expert', 'replica')), may hold values from 0.1 to 1
- expert_ids: int32 [16384, 4], P(('expert', 'replica')), may hold values from 0 to 31, all different within a row; in each aligned block of 128 rows (0 to 127, 128 to 255, ...) at most 24 rows name the same one
- gate_pre: bfloat16 [32, 3072, 1024], P('expert', 'replica', 'tensor'), may hold values from -6 to 6
- up_pre: bfloat16 [32, 3072, 1024], P('expert', 'replica', 'tensor'), may hold values from -6 to 6
- w_gate: bfloat16 [32, 3584, 1024], P('expert', 'replica', 'tensor'), may hold values from -0.09375 to 0.09375
- w_up: bfloat16 [32, 3584, 1024], P('expert', 'replica', 'tensor'), may hold values from -0.09375 to 0.09375
- w_down: bfloat16 [32, 3584, 1024], P('expert', 'replica', 'tensor'), may hold values from -0.09375 to 0.09375
- residual: bfloat16 [32, 14336, 1024], P('expert', 'replica', 'tensor'), may hold values from -6 to 6
Outputs:
- grad_in: bfloat16 [16384, 3584], P(('expert', 'replica'), 'tensor')
- code_sums: float32 [32, 3584, 1024], P('expert', 'replica', 'tensor')
- block_scales: float32 [32, 28, 1024], P('expert', None, 'tensor')
The draws below stay inside these ranges and needn't reach their ends.
Inputs may be any that keep to these rules, and one draw needn't show every extreme that they name: `expert_ids`: among the 128 tokens of one device no expert is named more than 24 times, and in every draw some device names some expert exactly 24 times; a token names 4 different experts.
All inputs are finite; a program needn't handle non-finite values.
Results may differ from the reference program's by a relative error of at most 0.017.
Values may be sent and summed in bfloat16 or wider, within the bound.
A program may use at most 128 MiB of HBM per device.

```python
import math
import jax
import jax.numpy as jnp
import numpy as np
from jax import lax

D = 3584
FF = 1024
BLOCK = 128
TOP = 4
TOK_DEV = 128
EXPERTS = 32
CAP = 24
SLOTS = 768
TOKENS = 16384
SAVED_ROWS = 3072
ERR_ROWS = 14336
N_REPLICA = 4
N_TENSOR = 2


def steps_of(stream_key, extent, split, least, high):
    loudness = 1.0
    for dim, blocks in split:
        steps = jax.random.uniform(jax.random.fold_in(jax.random.fold_in(stream_key, 6), dim), (blocks,), jnp.float32, least / len(split), high / len(split))
        loudness = loudness * jnp.repeat(jnp.exp(steps), extent[dim] // blocks).reshape((-1,) + (1,) * (len(extent) - 1 - dim))
    return loudness


def routed_block(stream_key, own, number, rows, number_of, top, most, lean):
    sequence = jax.random.permutation(stream_key, number_of)
    heavy_load, ordinary = portions_of(number_of, rows * top, most, lean, True), portions_of(number_of, rows * top, most, lean, False)
    places = jnp.arange(number_of)

    def named(sizes, offset_by):
        used = int((sizes > 0).sum())
        fixed = max(1, used // 4)
        passed = fixed + (places - fixed + offset_by * (used - fixed)) % max(1, number_of - fixed)
        return jnp.zeros((number_of,), jnp.int32).at[sequence[jnp.where(places < fixed, places, passed)]].set(jnp.asarray(sizes, jnp.int32))

    sizes = jnp.where(number % 4 == 0, named(heavy_load, number // 4), named(ordinary, number - number // 4 - 1))
    mixed = jax.random.permutation(jax.random.fold_in(own, 3), number_of)
    donor, taker = mixed[0:number_of // 2 * 2:2], mixed[1:number_of // 2 * 2:2]
    slack = jnp.minimum(sizes[donor] - 1, most - sizes[taker]) // 2
    slack = jnp.where((donor == sequence[0]) | (taker == sequence[0]) | (sizes[taker] == 0), 0, jnp.maximum(slack, 0))
    passed = jax.random.randint(jax.random.fold_in(own, 4), (number_of // 2,), 0, 1 << 20) % (slack + 1)
    sizes = sizes.at[donor].add(-passed).at[taker].add(passed)
    items = jnp.searchsorted(jnp.cumsum(sizes), jnp.arange(rows * top), side="right").astype(jnp.int32)
    table = items.reshape(top, rows).T
    table = table[jax.random.permutation(jax.random.fold_in(own, 1), rows)]
    offset_by = jax.random.randint(jax.random.fold_in(own, 2), (rows, 1), 0, top)
    return jnp.take_along_axis(table, (jnp.arange(top)[None, :] + offset_by) % top, axis=1)


def portions_of(amount, total, bound, slope, full):
    portions = [(1 << 20) // math.isqrt(standing ** slope) + 1 for standing in range(1, amount + 1)]
    largest = bound if full else min(bound, max(-(-total // amount), total * portions[0] // sum(portions)))
    least = 1 if total - largest >= amount - 1 else 0
    given, surplus = [largest] + [least] * (amount - 1), total - largest - least * (amount - 1)
    while surplus > 0:
        movable = [i for i in range(1, amount) if given[i] < largest] or [i for i in range(1, amount) if given[i] < bound]
        pool, budget = sum([portions[i] for i in movable]), surplus
        for i in movable:
            addition = min(bound - given[i], max(1, budget * portions[i] // pool), surplus)
            given[i] = given[i] + addition
            surplus = surplus - addition
    return np.array(given)


def bell_draw(own_key, shape, deviation, reach, split=(), held_as=jnp.bfloat16):
    values = deviation * jax.random.normal(own_key, shape, jnp.float32)
    if split:
        values = values * steps_of(own_key, shape, split, -0.22, 0.18)
    return jnp.clip(values, -reach, reach).astype(held_as)


def setup_inputs(seed: int = 0) -> dict:
    splits = jax.random.split(jax.random.key(seed), 10)
    grad_out = bell_draw(splits[0], (TOKENS, D), 1.0, 6.0, ((0, 128),))
    gates = jnp.clip(0.1 + 0.9 * jax.random.uniform(splits[1], (TOKENS, TOP), jnp.float32) ** steps_of(splits[1], (TOKENS, TOP), ((0, 128),), -0.2, 0.2), 0.1, 1.0)
    expert_ids_keys = jax.random.split(jax.random.fold_in(splits[2], 1), TOKENS // TOK_DEV)
    expert_ids_turns = jax.random.permutation(jax.random.fold_in(splits[2], 3), TOKENS // TOK_DEV)
    expert_ids = jax.vmap(lambda own, number: routed_block(jax.random.fold_in(splits[2], 2), own, number, TOK_DEV, EXPERTS, TOP, CAP, 2))(expert_ids_keys, expert_ids_turns).reshape((TOKENS, TOP))
    gate_pre = bell_draw(splits[3], (EXPERTS, SAVED_ROWS, FF), 1.0, 6.0, ((0, 32), (1, 4), (2, 2)))
    up_pre = bell_draw(splits[4], (EXPERTS, SAVED_ROWS, FF), 1.0, 6.0, ((0, 32), (1, 4), (2, 2)))
    w_gate = bell_draw(splits[5], (EXPERTS, D, FF), D ** -0.5, 0.09375, ((0, 32), (1, 4), (2, 2)))
    w_up = bell_draw(splits[6], (EXPERTS, D, FF), D ** -0.5, 0.09375, ((0, 32), (1, 4), (2, 2)))
    w_down = bell_draw(splits[7], (EXPERTS, D, FF), D ** -0.5, 0.09375, ((0, 32), (1, 4), (2, 2)))
    residual = bell_draw(splits[8], (EXPERTS, ERR_ROWS, FF), 1.5, 6.0, ((0, 32), (1, 4), (2, 2)))
    return dict(grad_out=grad_out, gates=gates, expert_ids=expert_ids, gate_pre=gate_pre, up_pre=up_pre, w_gate=w_gate, w_up=w_up, w_down=w_down, residual=residual)


def reference(grad_out, gates, expert_ids, gate_pre, up_pre, w_gate, w_up, w_down, residual):
    block_count = TOKENS // TOK_DEV
    pick_count = TOK_DEV * TOP
    route_ids = expert_ids.reshape(block_count, pick_count)
    onehot = (route_ids[:, :, None] == jnp.arange(EXPERTS, dtype=jnp.int32)[None, None, :]).astype(jnp.int32)
    earlier = jnp.cumsum(onehot, axis=1) - onehot
    slot_index = jnp.sum(earlier * onehot, axis=2)
    target = route_ids * CAP + slot_index
    filler = jnp.arange(pick_count, dtype=jnp.int32)
    slot_owner = jax.vmap(lambda places: jnp.full((EXPERTS * CAP,), -1, jnp.int32).at[places].set(filler))(target)
    gate_flat = gates.reshape(block_count, pick_count)
    group_width = FF // N_TENSOR

    def one_expert(grad_total, expert_id):
        gate_matrix = w_gate[expert_id]
        up_matrix = w_up[expert_id]
        down_matrix = w_down[expert_id]
        corrected_list = []
        maxima = []
        for replica_id in range(N_REPLICA):
            sources = jnp.arange(EXPERTS, dtype=jnp.int32) * N_REPLICA + replica_id
            owners = lax.dynamic_slice_in_dim(slot_owner[sources], expert_id * CAP, CAP, 1)
            filled = owners >= 0
            chosen = jnp.maximum(owners, 0)
            token_index = (sources[:, None] * TOK_DEV + chosen // TOP).reshape(-1)
            weight = jnp.where(filled, jnp.take_along_axis(gate_flat[sources], chosen, axis=1), 0.0).reshape(-1)
            routed = (grad_out[token_index].astype(jnp.float32) * weight[:, None]).astype(jnp.bfloat16)
            act_gate = lax.dynamic_slice_in_dim(gate_pre[expert_id], replica_id * SLOTS, SLOTS, 0).astype(jnp.float32)
            act_up = lax.dynamic_slice_in_dim(up_pre[expert_id], replica_id * SLOTS, SLOTS, 0).astype(jnp.float32)
            sigmoid_gate = jax.nn.sigmoid(act_gate)
            silu_gate = act_gate * sigmoid_gate
            hidden = (silu_gate * act_up).astype(jnp.bfloat16)
            hidden_grad = jnp.dot(routed, down_matrix, preferred_element_type=jnp.float32)
            gate_grad = (hidden_grad * act_up * sigmoid_gate * (1.0 + act_gate * (1.0 - sigmoid_gate))).astype(jnp.bfloat16)
            up_grad = (hidden_grad * silu_gate).astype(jnp.bfloat16)
            returned = jnp.zeros((SLOTS, D), jnp.float32)
            for group_id in range(N_TENSOR):
                lower = group_id * group_width
                upper = lower + group_width
                partial_value = jnp.dot(gate_grad[:, lower:upper], gate_matrix[:, lower:upper].T, preferred_element_type=jnp.float32)
                partial_value = partial_value + jnp.dot(up_grad[:, lower:upper], up_matrix[:, lower:upper].T, preferred_element_type=jnp.float32)
                returned = returned + lax.optimization_barrier(partial_value.astype(jnp.bfloat16)).astype(jnp.float32)
            returned = lax.optimization_barrier(returned.astype(jnp.bfloat16)).astype(jnp.float32)
            grad_total = grad_total.at[token_index].add(returned)
            weight_grad = jnp.dot(routed.T, hidden, preferred_element_type=jnp.float32)
            corrected = weight_grad + lax.dynamic_slice_in_dim(residual[expert_id], replica_id * D, D, 0).astype(jnp.float32)
            corrected_list.append(corrected)
            maxima.append(jnp.max(jnp.abs(corrected).reshape(D // BLOCK, BLOCK, FF), axis=1))
        largest = maxima[0]
        for other in maxima[1:]:
            largest = jnp.maximum(largest, other)
        block_scales = largest + 1e-6
        code_sums = jnp.zeros((D, FF), jnp.float32)
        for corrected in corrected_list:
            code = (corrected.reshape(D // BLOCK, BLOCK, FF) / block_scales[:, None, :]).astype(jnp.bfloat16)
            code_sums = code_sums + lax.optimization_barrier(code).astype(jnp.float32).reshape(D, FF)
        return grad_total, (code_sums, block_scales)

    grad_total, outputs = lax.scan(one_expert, jnp.zeros((TOKENS, D), jnp.float32), jnp.arange(EXPERTS, dtype=jnp.int32))
    return grad_total.astype(jnp.bfloat16), outputs[0], outputs[1]
```

```python
import jax
import jax.numpy as jnp
from jax import lax
from jax.experimental import pallas as pl
from jax.experimental.pallas import tpu as pltpu
from jax.sharding import PartitionSpec as P

MESH = pl.DeviceIdType.MESH
BF16, F32 = jnp.bfloat16, jnp.float32

EXPERTS, REPLICAS = 32, 4
TOKENS, TOP, CAP = 128, 4, 24
D, GROUP, SHARD, BLOCK = 3584, 512, 896, 128
HALF_D = D // 2
ROWS_A, ROWS_B = EXPERTS * 16, EXPERTS * 8
SLOTS = ROWS_A + ROWS_B
WIDE = 3 * SHARD
CUT = SHARD // 2


def dot(a, b, dims=((1,), (0,))):
    return lax.dot_general(a, b, (dims, ((), ())), preferred_element_type=F32)


def kernel(
    ids_ref, gates_ref, grad_hbm, gate_hbm, up_hbm, wg_hbm, wu_hbm, wd_hbm, res_hbm,
    grad_in_ref, sums_ref, scales_ref,
    out, rcv, ret, part_send, part_got, part_own, wf, routed_b, pick, pick_t, grad, gate_pre, up_pre,
    hid, fac_gate, fac_up, gate_grad, up_grad, res, corr, code_got, maxima,
    a_send, a_recv, f_send, f_recv, r_send, r_recv, w_send, w_recv, p_send, p_recv,
    m_send, m_recv, c_send, c_recv, l_sem,
):
    me = lax.axis_index("expert")
    y = lax.axis_index("replica")
    core = lax.axis_index("tensor")
    other = 1 - core
    right, left, opposite = lax.rem(y + 1, 4), lax.rem(y + 3, 4), lax.rem(y + 2, 4)
    weights = (wd_hbm, wg_hbm, wu_hbm)

    def local_copies():
        copies = [
            pltpu.make_async_copy(
                grad_hbm.at[:, pl.ds(pl.multiple_of(core * HALF_D, HALF_D), HALF_D)], grad, l_sem.at[0]
            ),
            pltpu.make_async_copy(gate_hbm, gate_pre, l_sem.at[1]),
            pltpu.make_async_copy(up_hbm, up_pre, l_sem.at[2]),
            pltpu.make_async_copy(res_hbm, res, l_sem.at[3]),
        ]
        for w in range(3):
            copies.append(pltpu.make_async_copy(weights[w], wf.at[w, y], l_sem.at[4 + w]))
        return copies

    locals_ = local_copies()
    for copy in locals_:
        copy.start()

    barrier = pltpu.get_barrier_semaphore()

    def greet(i, _):
        pl.semaphore_signal(
            barrier, inc=1, device_id={"expert": lax.rem(me + i, EXPERTS)}, device_id_type=MESH
        )
        return 0

    lax.fori_loop(1, EXPERTS, greet, 0)
    for peer in (right, left, opposite):
        pl.semaphore_signal(barrier, inc=1, device_id={"replica": peer}, device_id_type=MESH)
    pl.semaphore_signal(barrier, inc=1, device_id={"tensor": other}, device_id_type=MESH)

    ids = ids_ref[...].astype(F32)
    expert_row = lax.broadcasted_iota(jnp.int32, (EXPERTS, TOKENS), 0).astype(F32)
    named = jnp.zeros((EXPERTS, TOKENS), F32)
    for k in range(TOP):
        named = named + jnp.where(ids[k : k + 1, :] == expert_row, 1.0, 0.0)
    before = jnp.where(
        lax.broadcasted_iota(jnp.int32, (TOKENS, TOKENS), 0)
        < lax.broadcasted_iota(jnp.int32, (TOKENS, TOKENS), 1),
        1.0,
        0.0,
    ).astype(BF16)
    earlier = dot(named.astype(BF16), before)
    keys = []
    for k in range(TOP):
        id_k = ids[k : k + 1, :]
        slot_k = jnp.sum(jnp.where(id_k == expert_row, earlier, 0.0), axis=0, keepdims=True)
        keys.append(id_k * 32.0 + slot_k)
    row = lax.broadcasted_iota(jnp.int32, (ROWS_A, 1), 0)
    in_row = lax.rem(row, 16)
    base = (row - in_row) * 2
    key_a = (base + in_row).astype(F32)
    key_b = (base + 16 + lax.rem(row, 8)).astype(F32)
    lower = in_row < 8
    hot = jnp.zeros((ROWS_A, TOKENS), F32)
    weigh = jnp.zeros((ROWS_A, TOKENS), F32)
    hot_b = jnp.zeros((ROWS_A, TOKENS), F32)
    weigh_b = jnp.zeros((ROWS_A, TOKENS), F32)
    for k in range(TOP):
        same = key_a == keys[k]
        same_b = key_b == keys[k]
        gate_k = gates_ref[k : k + 1, :]
        hot = hot + jnp.where(same, 1.0, 0.0)
        weigh = weigh + jnp.where(same, gate_k, 0.0)
        hot_b = hot_b + jnp.where(same_b, 1.0, 0.0)
        weigh_b = weigh_b + jnp.where(same_b, gate_k, 0.0)
    gate_a = jnp.sum(weigh, axis=1, keepdims=True)
    gate_b = jnp.sum(weigh_b, axis=1, keepdims=True)
    hot_b0 = jnp.where(lower, hot_b, 0.0)
    hot_b1 = jnp.where(lower, 0.0, hot_b)
    pick[0] = hot.astype(BF16)
    pick[1] = hot_b0.astype(BF16)
    pick[2] = hot_b1.astype(BF16)

    def weight_copy(w, i):
        peer, lo = ((right, 0), (left, CUT), (right, CUT), (left, 0))[i]
        return pltpu.make_async_remote_copy(
            src_ref=weights[w].at[pl.ds(lo, CUT)],
            dst_ref=wf.at[w, y, pl.ds(lo, CUT)],
            send_sem=w_send.at[w * 6 + i],
            recv_sem=w_recv.at[w * 6 + i],
            device_id={"replica": peer},
            device_id_type=MESH,
        )

    def weight_relay(w, i):
        peer, owner, lo = ((right, left, 0), (left, right, CUT))[i]
        block = wf.at[w, owner, pl.ds(lo, CUT)]
        return pltpu.make_async_remote_copy(
            src_ref=block,
            dst_ref=block,
            send_sem=w_send.at[w * 6 + 4 + i],
            recv_sem=w_recv.at[w * 6 + 4 + i],
            device_id={"replica": peer},
            device_id_type=MESH,
        )

    def relay(w):
        for i in range(2):
            weight_copy(w, i).wait_recv()
            weight_relay(w, i).start()

    def weight_ready(w):
        locals_[4 + w].wait()
        for i in (2, 3):
            weight_copy(w, i).wait_recv()
        for i in range(2):
            weight_relay(w, i).wait_recv()

    pl.semaphore_wait(barrier, EXPERTS + 3)
    for w in range(3):
        for i in range(4):
            weight_copy(w, i).start()

    locals_[0].wait()
    for q in range(4):
        rows = pl.ds(q * 128, 128)
        block = dot(pick[0, rows, :], grad[...]) * gate_a[q * 128 : (q + 1) * 128]
        out[pl.ds(q * 8, 8), :, 0:HALF_D] = block.astype(BF16).reshape(8, 16, HALF_D)
        block = dot(pick[1, rows, :], grad[:, 0:SHARD]) + dot(pick[2, rows, :], grad[:, SHARD:HALF_D])
        block = block * gate_b[q * 128 : (q + 1) * 128]
        out[pl.ds(q * 8, 8), :, HALF_D:WIDE] = block.astype(BF16).reshape(8, 16, SHARD)

    def dispatch(i):
        peer = lax.rem(me + i, EXPERTS)
        return pltpu.make_async_remote_copy(
            src_ref=out.at[peer],
            dst_ref=rcv.at[core, me],
            send_sem=a_send.at[i],
            recv_sem=a_recv.at[i],
            device_id={"expert": peer},
            device_id_type=MESH,
        )

    def share(i):
        source = lax.rem(me + EXPERTS - i, EXPERTS)
        return pltpu.make_async_remote_copy(
            src_ref=rcv.at[core, source],
            dst_ref=rcv.at[core, source],
            send_sem=f_send.at[i],
            recv_sem=f_recv.at[i],
            device_id={"tensor": other},
            device_id_type=MESH,
        )

    def start_dispatch(i, _):
        dispatch(i).start()
        return 0

    lax.fori_loop(1, EXPERTS, start_dispatch, 0)
    own = pltpu.make_async_copy(out.at[me], rcv.at[core, me], l_sem.at[7])
    own.start()

    locals_[1].wait()
    locals_[2].wait()

    def activate(g, _):
        rows = pl.ds(pl.multiple_of(g * 192, 192), 192)
        a = gate_pre[rows, :].astype(F32).reshape(8, CAP, GROUP)
        u = up_pre[rows, :].astype(F32).reshape(8, CAP, GROUP)
        for lo, hi, at in ((0, 16, g * 128), (16, 24, ROWS_A + g * 64)):
            n = 8 * (hi - lo)
            a_part = a[:, lo:hi].reshape(n, GROUP)
            u_part = u[:, lo:hi].reshape(n, GROUP)
            sigma = 1.0 / (1.0 + jnp.exp(-a_part))
            silu = a_part * sigma
            to = pl.ds(pl.multiple_of(at, 64), n)
            hid[to, :] = (silu * u_part).astype(BF16)
            fac_up[to, :] = silu
            fac_gate[to, :] = u_part * sigma * (1.0 + a_part * (1.0 - sigma))
        return 0

    lax.fori_loop(0, 4, activate, 0)
    for j in range(3):
        pick_t[j] = jnp.transpose(pick[j].astype(F32)).astype(BF16)

    own.wait()
    share(0).start()

    def pass_on(i, _):
        dispatch(i).wait_recv()
        share(i).start()
        return 0

    relay(0)
    lax.fori_loop(1, 12, pass_on, 0)
    relay(1)
    lax.fori_loop(12, 24, pass_on, 0)
    relay(2)
    lax.fori_loop(24, EXPERTS, pass_on, 0)

    def share_got(i, _):
        share(i).wait()
        return 0

    lax.fori_loop(0, EXPERTS, share_got, 0)

    for h in range(2):
        for q in range(2):
            def unfold(g, _, h=h, q=q):
                raw = rcv[h, pl.ds(g * 8, 8), :, HALF_D:WIDE].astype(F32)
                rows = raw.reshape(8, 2, 8, SHARD)[:, q].reshape(64, SHARD)
                routed_b[h, pl.ds(pl.multiple_of(g * 64, 64), 64), q * SHARD : (q + 1) * SHARD] = rows.astype(BF16)
                return 0

            lax.fori_loop(0, 4, unfold, 0)

    def w_half(w, h):
        return wf[w, pl.ds(2 * h, 2)].reshape(HALF_D, GROUP)

    weight_ready(0)

    def grads(at, total):
        rows = pl.ds(pl.multiple_of(at, 256), 256)
        gate_grad[rows, :] = (total * fac_gate[rows, :]).astype(BF16)
        up_grad[rows, :] = (total * fac_up[rows, :]).astype(BF16)

    def rows_a(t, _):
        total = jnp.zeros((256, GROUP), F32)
        for h in range(2):
            x = rcv[h, pl.ds(t * 16, 16), :, 0:HALF_D].reshape(256, HALF_D)
            total = total + dot(x, w_half(0, h))
        grads(t * 256, total)
        return 0

    lax.fori_loop(0, 2, rows_a, 0)
    grads(ROWS_A, dot(routed_b[0], w_half(0, 0)) + dot(routed_b[1], w_half(0, 1)))

    locals_[3].wait()
    for h in range(2):
        def correct(t, _, h=h):
            columns = pl.ds(pl.multiple_of(t * 256, 256), 256)
            x = rcv[h, :, :, columns].reshape(ROWS_A, 256)
            total = dot(x, hid[0:ROWS_A, :], ((0,), (0,)))
            total = total + dot(routed_b[h, :, columns], hid[ROWS_A:SLOTS, :], ((0,), (0,)))
            rows = pl.ds(pl.multiple_of(h * HALF_D + t * 256, 256), 256)
            total = total + res[rows, :].astype(F32)
            corr[rows, :] = total
            for b in range(2):
                top = jnp.max(jnp.abs(total[b * BLOCK : (b + 1) * BLOCK]), axis=0, keepdims=True)
                maxima[y, pl.ds(h * 14 + t * 2 + b, 1), :] = top
            return 0

        lax.fori_loop(0, 7, correct, 0)

    def max_copy(i):
        return pltpu.make_async_remote_copy(
            src_ref=maxima.at[y],
            dst_ref=maxima.at[y],
            send_sem=m_send.at[i],
            recv_sem=m_recv.at[i],
            device_id={"replica": (right, left, opposite)[i]},
            device_id_type=MESH,
        )

    for i in range(3):
        max_copy(i).start()
    for i in range(3):
        max_copy(i).wait()
    largest = jnp.maximum(jnp.maximum(maxima[0], maxima[1]), jnp.maximum(maxima[2], maxima[3]))
    scales_ref[...] = largest + 1e-6

    def code(b, _):
        rows = pl.ds(pl.multiple_of(b * BLOCK, BLOCK), BLOCK)
        res[rows, :] = (corr[rows, :] / scales_ref[pl.ds(b, 1), :]).astype(BF16)
        return 0

    lax.fori_loop(0, D // BLOCK, code, 0)

    weight_ready(1)
    weight_ready(2)

    def code_copy(i):
        peer = (right, left, opposite)[i]
        return pltpu.make_async_remote_copy(
            src_ref=res.at[pl.ds(pl.multiple_of(peer * SHARD, SHARD), SHARD)],
            dst_ref=code_got.at[i],
            send_sem=c_send.at[i],
            recv_sem=c_recv.at[i],
            device_id={"replica": peer},
            device_id_type=MESH,
        )

    for i in range(3):
        code_copy(i).start()

    def partial(h, dst):
        def tile(t, _):
            rows = pl.ds(pl.multiple_of(t * 256, 256), 256)
            for q in range(2):
                s = 2 * h + q
                value = dot(gate_grad[rows, :], wf[1, s], ((1,), (1,))) + dot(
                    up_grad[rows, :], wf[2, s], ((1,), (1,))
                )
                dst[pl.ds(t * 16, 16), :, q * SHARD : (q + 1) * SHARD] = value.astype(BF16).reshape(
                    16, 16, SHARD
                )
            return 0

        lax.fori_loop(0, 2, tile, 0)

        def tile_b(t, _):
            rows = pl.ds(pl.multiple_of(ROWS_A + t * 128, 128), 128)
            values = []
            for q in range(2):
                s = 2 * h + q
                value = dot(gate_grad[rows, :], wf[1, s], ((1,), (1,))) + dot(
                    up_grad[rows, :], wf[2, s], ((1,), (1,))
                )
                values.append(value.reshape(16, 1, 8, SHARD))
            both = jnp.concatenate(values, axis=1).reshape(16, 16, SHARD)
            dst[pl.ds(t * 16, 16), :, HALF_D:WIDE] = both.astype(BF16)
            return 0

        lax.fori_loop(0, 2, tile_b, 0)

    partial(other, part_send)
    swap = pltpu.make_async_remote_copy(
        src_ref=part_send,
        dst_ref=part_got,
        send_sem=p_send,
        recv_sem=p_recv,
        device_id={"tensor": other},
        device_id_type=MESH,
    )
    swap.start()
    partial(core, part_own)

    def dispatched(i, _):
        dispatch(i).wait_send()
        return 0

    lax.fori_loop(1, EXPERTS, dispatched, 0)
    swap.wait()

    def give_back(i):
        peer = lax.rem(me + i, EXPERTS)
        return pltpu.make_async_remote_copy(
            src_ref=out.at[peer],
            dst_ref=ret.at[me],
            send_sem=r_send.at[i],
            recv_sem=r_recv.at[i],
            device_id={"expert": peer},
            device_id_type=MESH,
        )

    def summed(e):
        return (part_own[e].astype(F32) + part_got[e].astype(F32)).astype(BF16)

    def start_back(i, _):
        e = lax.rem(me + i, EXPERTS)
        out[e] = summed(e)
        give_back(i).start()
        return 0

    lax.fori_loop(1, EXPERTS, start_back, 0)
    ret[me] = summed(me)

    for i in range(3):
        code_copy(i).wait()

    def add_codes(t, _):
        rows = pl.ds(pl.multiple_of(t * 128, 128), 128)
        total = res[pl.ds(pl.multiple_of(y * SHARD + t * 128, 128), 128), :].astype(F32)
        for i in range(3):
            total = total + code_got[i, rows, :].astype(F32)
        sums_ref[rows, :] = total
        return 0

    lax.fori_loop(0, SHARD // 128, add_codes, 0)

    def came_back(i, _):
        give_back(i).wait()
        return 0

    lax.fori_loop(1, EXPERTS, came_back, 0)
    back_b = ret[:, :, HALF_D:WIDE].reshape(ROWS_A, SHARD)
    for q in range(2):
        columns = slice(q * SHARD, (q + 1) * SHARD)
        total = dot(pick_t[0], ret[:, :, columns].reshape(ROWS_A, SHARD)) + dot(pick_t[1 + q], back_b)
        grad_in_ref[:, columns] = total.astype(BF16)

    for w in range(3):
        for i in range(4):
            weight_copy(w, i).wait_send()
        for i in range(2):
            weight_relay(w, i).wait_send()


def local(grad_out, gates, expert_ids, gate_pre, up_pre, w_gate, w_up, w_down, residual):
    whole = pl.BlockSpec(memory_space=pltpu.VMEM)
    hbm = pl.BlockSpec(memory_space=pl.ANY)
    message = (EXPERTS, 16, WIDE)
    dma = pltpu.SemaphoreType.DMA
    grad_in, code_sums, scales = pl.pallas_call(
        kernel,
        out_shape=(
            jax.ShapeDtypeStruct((TOKENS, HALF_D), BF16),
            jax.ShapeDtypeStruct((SHARD, GROUP), F32),
            jax.ShapeDtypeStruct((D // BLOCK, GROUP), F32),
        ),
        in_specs=[whole, whole] + [hbm] * 7,
        out_specs=(whole, whole, whole),
        scratch_shapes=[
            pltpu.VMEM(message, BF16),
            pltpu.VMEM((2,) + message, BF16),
            pltpu.VMEM(message, BF16),
            pltpu.VMEM(message, BF16),
            pltpu.VMEM(message, BF16),
            pltpu.VMEM(message, BF16),
            pltpu.VMEM((3, REPLICAS, SHARD, GROUP), BF16),
            pltpu.VMEM((2, ROWS_B, HALF_D), BF16),
            pltpu.VMEM((3, ROWS_A, TOKENS), BF16),
            pltpu.VMEM((3, TOKENS, ROWS_A), BF16),
            pltpu.VMEM((TOKENS, HALF_D), BF16),
            pltpu.VMEM((SLOTS, GROUP), BF16),
            pltpu.VMEM((SLOTS, GROUP), BF16),
            pltpu.VMEM((SLOTS, GROUP), BF16),
            pltpu.VMEM((SLOTS, GROUP), F32),
            pltpu.VMEM((SLOTS, GROUP), F32),
            pltpu.VMEM((SLOTS, GROUP), BF16),
            pltpu.VMEM((SLOTS, GROUP), BF16),
            pltpu.VMEM((D, GROUP), BF16),
            pltpu.VMEM((D, GROUP), F32),
            pltpu.VMEM((3, SHARD, GROUP), BF16),
            pltpu.VMEM((REPLICAS, D // BLOCK, GROUP), F32),
            dma((EXPERTS,)),
            dma((EXPERTS,)),
            dma((EXPERTS,)),
            dma((EXPERTS,)),
            dma((EXPERTS,)),
            dma((EXPERTS,)),
            dma((18,)),
            dma((18,)),
            dma,
            dma,
            dma((3,)),
            dma((3,)),
            dma((3,)),
            dma((3,)),
            dma((8,)),
        ],
        compiler_params=pltpu.CompilerParams(
            collective_id=0, has_side_effects=True, vmem_limit_bytes=62 * 2**20
        ),
        cost_estimate=pl.CostEstimate(flops=11_300_000_000, bytes_accessed=14_000_000, transcendentals=400_000),
    )(
        expert_ids.T, gates.T, grad_out, gate_pre[0], up_pre[0], w_gate[0], w_up[0], w_down[0], residual[0]
    )
    return grad_in, code_sums[None], scales[None]


def solution(mesh):
    spec = P("expert", "replica", "tensor")
    tokens = P(("expert", "replica"), None)
    in_specs = (tokens,) * 3 + (spec,) * 6
    out_specs = (P(("expert", "replica"), "tensor"), spec, P("expert", None, "tensor"))
    return jax.shard_map(local, mesh=mesh, in_specs=in_specs, out_specs=out_specs, check_vma=False)
```

```python
import jax
import jax.numpy as jnp
from jax import lax
from jax.experimental import pallas as pl
from jax.experimental.pallas import tpu as pltpu
from jax.sharding import PartitionSpec as P

MESH = pl.DeviceIdType.MESH
BF16, F32 = jnp.bfloat16, jnp.float32

EXPERTS, REPLICAS = 32, 4
TOKENS, TOP, CAP = 128, 4, 24
D, GROUP, SHARD, BLOCK = 3584, 512, 896, 128
HALF_D = D // 2
ROWS_A, ROWS_B = EXPERTS * 16, EXPERTS * 8
SLOTS = ROWS_A + ROWS_B
WIDE = 3 * SHARD
CUT = SHARD // 2
TILE = 8 * CAP


def dot(a, b, dims=((1,), (0,))):
    return lax.dot_general(a, b, (dims, ((), ())), preferred_element_type=F32)


def kernel(
    ids_ref, gates_ref, grad_hbm, gate_hbm, up_hbm, wg_hbm, wu_hbm, wd_hbm, res_hbm,
    grad_in_ref, sums_ref, scales_ref,
    out, rcv, ret, part, part_got, wf, routed, pick, pick_t, grad, gate_pre, up_pre,
    hid, fac_gate, fac_up, gate_grad, up_grad, res, corr, code_got, maxima, total_in,
    a_send, a_recv, f_send, f_recv, r_send, r_recv, w_send, w_recv, p_send, p_recv,
    m_send, m_recv, c_send, c_recv, l_sem,
):
    me = lax.axis_index("expert")
    y = lax.axis_index("replica")
    core = lax.axis_index("tensor")
    other = 1 - core
    odd = lax.rem(y, 2)
    near = lax.div(y, 2)
    pair = y + 1 - 2 * odd
    next_ = lax.rem(y + 3 + 2 * odd, REPLICAS)
    opposite = lax.rem(y + 2, REPLICAS)
    weights = (wd_hbm, wg_hbm, wu_hbm)

    def saved(s):
        source = lax.rem(me + EXPERTS - s, EXPERTS)
        return (
            pltpu.make_async_copy(gate_hbm.at[source], gate_pre.at[s], l_sem.at[1]),
            pltpu.make_async_copy(up_hbm.at[source], up_pre.at[s], l_sem.at[2]),
        )

    grad_copy = pltpu.make_async_copy(
        grad_hbm.at[:, pl.ds(pl.multiple_of(core * HALF_D, HALF_D), HALF_D)], grad, l_sem.at[0]
    )
    res_copy = pltpu.make_async_copy(res_hbm, res, l_sem.at[3])
    own_weights = [pltpu.make_async_copy(weights[w], wf.at[w, y], l_sem.at[4 + w]) for w in range(3)]
    grad_copy.start()

    barrier = pltpu.get_barrier_semaphore()

    def greet(i, _):
        pl.semaphore_signal(
            barrier, inc=1, device_id={"expert": lax.rem(me + i, EXPERTS)}, device_id_type=MESH
        )
        return 0

    for peer in (pair, next_, opposite):
        pl.semaphore_signal(barrier, inc=1, device_id={"replica": peer}, device_id_type=MESH)
    pl.semaphore_signal(barrier, inc=1, device_id={"tensor": other}, device_id_type=MESH)
    lax.fori_loop(1, EXPERTS, greet, 0)

    def start_saved(s, _):
        for copy in saved(s):
            copy.start()
        return 0

    lax.fori_loop(0, EXPERTS, start_saved, 0)
    for copy in own_weights:
        copy.start()
    res_copy.start()

    ids = ids_ref[...].astype(F32)
    expert_row = lax.broadcasted_iota(jnp.int32, (EXPERTS, TOKENS), 0).astype(F32)
    named = jnp.zeros((EXPERTS, TOKENS), F32)
    for k in range(TOP):
        named = named + jnp.where(ids[k : k + 1, :] == expert_row, 1.0, 0.0)
    before = jnp.where(
        lax.broadcasted_iota(jnp.int32, (TOKENS, TOKENS), 0)
        < lax.broadcasted_iota(jnp.int32, (TOKENS, TOKENS), 1),
        1.0,
        0.0,
    ).astype(BF16)
    earlier = dot(named.astype(BF16), before)
    keys = []
    for k in range(TOP):
        id_k = ids[k : k + 1, :]
        slot_k = jnp.sum(jnp.where(id_k == expert_row, earlier, 0.0), axis=0, keepdims=True)
        keys.append(id_k * 32.0 + slot_k)
    row = lax.broadcasted_iota(jnp.int32, (ROWS_A, 1), 0)
    in_row = jnp.bitwise_and(row, 15)
    base = jnp.bitwise_and(me + jnp.right_shift(row, 4), EXPERTS - 1) * 32
    key_a = (base + in_row).astype(F32)
    key_b = (base + 16 + jnp.bitwise_and(row, 7)).astype(F32)
    lower = in_row < 8
    hot = jnp.zeros((ROWS_A, TOKENS), F32)
    weigh = jnp.zeros((ROWS_A, TOKENS), F32)
    hot_b = jnp.zeros((ROWS_A, TOKENS), F32)
    weigh_b = jnp.zeros((ROWS_A, TOKENS), F32)
    for k in range(TOP):
        same = key_a == keys[k]
        same_b = key_b == keys[k]
        gate_k = gates_ref[k : k + 1, :]
        hot = hot + jnp.where(same, 1.0, 0.0)
        weigh = weigh + jnp.where(same, gate_k, 0.0)
        hot_b = hot_b + jnp.where(same_b, 1.0, 0.0)
        weigh_b = weigh_b + jnp.where(same_b, gate_k, 0.0)
    gate_a = jnp.sum(weigh, axis=1, keepdims=True)
    gate_b = jnp.sum(weigh_b, axis=1, keepdims=True)
    pick[0] = hot.astype(BF16)
    pick[1] = jnp.where(lower, hot_b, 0.0).astype(BF16)
    pick[2] = jnp.where(lower, 0.0, hot_b).astype(BF16)

    def weight_copy(number):
        if number < 12:
            w, lo = number % 6 // 2, number % 2 * CUT
            owner, peer = y, (pair if number < 6 else next_)
            src = weights[w].at[pl.ds(lo, CUT)]
        else:
            w, lo = ((0, 0), (0, CUT), (2, 0), (1, 0), (1, CUT), (2, CUT))[number - 12]
            owner, peer = (pair, next_) if number < 15 else (next_, pair)
            src = wf.at[w, owner, pl.ds(lo, CUT)]
        return pltpu.make_async_remote_copy(
            src_ref=src,
            dst_ref=wf.at[w, owner, pl.ds(lo, CUT)],
            send_sem=w_send.at[number],
            recv_sem=w_recv.at[number],
            device_id={"replica": peer},
            device_id_type=MESH,
        )

    def weights_start(*numbers):
        for number in numbers:
            weight_copy(number).start()

    def weights_wait(*numbers):
        for number in numbers:
            weight_copy(number).wait_recv()

    pl.semaphore_wait(barrier, EXPERTS + 3)
    weights_start(0, 6, 1, 7, 2, 3, 4, 5)

    def dispatch(s):
        return pltpu.make_async_remote_copy(
            src_ref=out.at[s],
            dst_ref=rcv.at[core, s],
            send_sem=a_send.at[s],
            recv_sem=a_recv.at[s],
            device_id={"expert": lax.rem(me + s, EXPERTS)},
            device_id_type=MESH,
        )

    def start_dispatch(s, _):
        dispatch(s).start()
        return 0

    grad_copy.wait()
    own = pltpu.make_async_copy(out.at[0], rcv.at[core, 0], l_sem.at[7])
    for q in range(4):
        rows = pl.ds(q * 128, 128)
        block = dot(pick[0, rows, :], grad[...]) * gate_a[q * 128 : (q + 1) * 128]
        out[pl.ds(q * 8, 8), :, 0:HALF_D] = block.astype(BF16).reshape(8, 16, HALF_D)
        block = dot(pick[1, rows, :], grad[:, 0:SHARD]) + dot(pick[2, rows, :], grad[:, SHARD:HALF_D])
        block = block * gate_b[q * 128 : (q + 1) * 128]
        out[pl.ds(q * 8, 8), :, HALF_D:WIDE] = block.astype(BF16).reshape(8, 16, SHARD)
        lax.fori_loop(max(1, q * 8), q * 8 + 8, start_dispatch, 0)
        if q == 0:
            own.start()

    def share(s):
        return pltpu.make_async_remote_copy(
            src_ref=rcv.at[core, s],
            dst_ref=rcv.at[core, s],
            send_sem=f_send.at[s],
            recv_sem=f_recv.at[s],
            device_id={"tensor": other},
            device_id_type=MESH,
        )

    def pass_on(s, _):
        dispatch(s).wait_recv()
        share(s).start()
        return 0

    def share_got(s, _):
        share(s).wait()
        return 0

    own.wait()
    share(0).start()

    pltpu.make_async_copy(gate_hbm, gate_pre, l_sem.at[1]).wait()
    pltpu.make_async_copy(up_hbm, up_pre, l_sem.at[2]).wait()

    def activate(g, _):
        a = gate_pre[pl.ds(g * 8, 8)].astype(F32)
        u = up_pre[pl.ds(g * 8, 8)].astype(F32)
        for lo, hi, at in ((0, 16, g * TILE), (16, 24, g * TILE + 128)):
            n = 8 * (hi - lo)
            a_part = a[:, lo:hi].reshape(n, GROUP)
            u_part = u[:, lo:hi].reshape(n, GROUP)
            sigma = 1.0 / (1.0 + jnp.exp(-a_part))
            silu = a_part * sigma
            to = pl.ds(pl.multiple_of(at, 64), n)
            hid[to, :] = (silu * u_part).astype(BF16)
            fac_up[to, :] = silu
            fac_gate[to, :] = u_part * sigma * (1.0 + a_part * (1.0 - sigma))
        return 0

    lax.fori_loop(0, 4, activate, 0)

    def tile_of(g):
        return pl.ds(pl.multiple_of(g * TILE, TILE), TILE)

    def unfold(g):
        lax.fori_loop(g * 8, g * 8 + 8, share_got, 0)
        for h in range(2):
            routed[h, g * TILE : g * TILE + 128, :] = rcv[h, g * 8 : g * 8 + 8, :, 0:HALF_D].reshape(128, HALF_D)
            raw = rcv[h, g * 8 : g * 8 + 8, :, HALF_D:WIDE].astype(F32).reshape(8, 2, 8, SHARD)
            for q in range(2):
                routed[h, g * TILE + 128 : (g + 1) * TILE, q * SHARD : (q + 1) * SHARD] = (
                    raw[:, q].reshape(64, SHARD).astype(BF16)
                )

    def w_half(w, h):
        return wf[w, pl.ds(2 * h, 2)].reshape(HALF_D, GROUP)

    def hidden_grads(g, _):
        rows = tile_of(g)
        total = dot(routed[0, rows, :], w_half(0, 0)) + dot(routed[1, rows, :], w_half(0, 1))
        gate_grad[rows, :] = (total * fac_gate[rows, :]).astype(BF16)
        up_grad[rows, :] = (total * fac_up[rows, :]).astype(BF16)
        return 0

    def correct(lo, hi, first, last):
        for h in range(2):
            def step(t, _, h=h):
                columns = pl.ds(pl.multiple_of(t * 256, 256), 256)
                rows = pl.ds(pl.multiple_of(h * HALF_D + t * 256, 256), 256)
                total = dot(routed[h, lo:hi, columns], hid[lo:hi, :], ((0,), (0,)))
                total = total + (res[rows, :].astype(F32) if first else corr[rows, :])
                corr[rows, :] = total
                if last:
                    for b in range(2):
                        top = jnp.max(jnp.abs(total[b * BLOCK : (b + 1) * BLOCK]), axis=0, keepdims=True)
                        maxima[y, pl.ds(h * 14 + t * 2 + b, 1), :] = top
                return 0

            lax.fori_loop(0, 7, step, 0)

    def swap(stage, g):
        block = pl.ds(g * 8, 8)
        return pltpu.make_async_remote_copy(
            src_ref=part.at[stage, block],
            dst_ref=part_got.at[block],
            send_sem=p_send.at[g],
            recv_sem=p_recv.at[g],
            device_id={"tensor": other},
            device_id_type=MESH,
        )

    def partial(stage):
        half = near if stage == 0 else 1 - near

        def group(g, _):
            rows = tile_of(g)
            values = []
            for q in range(2):
                s = 2 * half + q
                value = dot(gate_grad[rows, :], wf[1, s], ((1,), (1,))) + dot(
                    up_grad[rows, :], wf[2, s], ((1,), (1,))
                )
                part[stage, pl.ds(g * 8, 8), :, q * SHARD : (q + 1) * SHARD] = (
                    value[0:128].astype(BF16).reshape(8, 16, SHARD)
                )
                values.append(value[128:TILE].reshape(8, 1, 8, SHARD))
            both = jnp.concatenate(values, axis=1).reshape(8, 16, SHARD)
            part[stage, pl.ds(g * 8, 8), :, HALF_D:WIDE] = both.astype(BF16)

            @pl.when(half != core)
            def _():
                swap(stage, g).start()

            return 0

        return group

    def give_back(s):
        return pltpu.make_async_remote_copy(
            src_ref=out.at[s],
            dst_ref=ret.at[s],
            send_sem=r_send.at[s],
            recv_sem=r_recv.at[s],
            device_id={"expert": lax.rem(me + EXPERTS - s, EXPERTS)},
            device_id_type=MESH,
        )

    def send_back(stage, lo, hi):
        half = near if stage == 0 else 1 - near

        def summed(s):
            return (part[stage, s].astype(F32) + part_got[s].astype(F32)).astype(BF16)

        def one(s, _):
            dispatch(s).wait_send()
            out[s] = summed(s)
            give_back(s).start()
            return 0

        @pl.when(half == core)
        def _():
            for g in range(lo, hi):
                swap(stage, g).wait_recv()
                if g == 0:
                    ret[0] = summed(0)
                lax.fori_loop(max(1, g * 8), g * 8 + 8, one, 0)

    lax.fori_loop(1, 3, pass_on, 0)
    weights_wait(0)
    weights_start(12)
    lax.fori_loop(3, 6, pass_on, 0)
    weights_wait(1)
    weights_start(13, 8, 9, 11, 10)
    for j in range(3):
        pick_t[j] = jnp.transpose(pick[j].astype(F32)).astype(BF16)
    lax.fori_loop(6, 8, pass_on, 0)
    unfold(0)
    lax.fori_loop(8, 16, pass_on, 0)
    unfold(1)
    own_weights[0].wait()
    weights_wait(6, 7, 12, 13)
    lax.fori_loop(0, 2, hidden_grads, 0)
    lax.fori_loop(16, 24, pass_on, 0)
    unfold(2)
    hidden_grads(2, 0)
    res_copy.wait()
    correct(0, 3 * TILE, True, False)
    weights_wait(8, 4)
    weights_start(15, 14)
    lax.fori_loop(24, EXPERTS, pass_on, 0)
    weights_wait(9)
    weights_start(16)
    own_weights[1].wait()
    own_weights[2].wait()
    weights_wait(2, 3, 5)
    lax.fori_loop(0, 3, partial(0), 0)
    unfold(3)
    hidden_grads(3, 0)
    partial(0)(3, 0)
    send_back(0, 0, 4)

    correct(3 * TILE, SLOTS, False, True)

    def max_copy(i):
        return pltpu.make_async_remote_copy(
            src_ref=maxima.at[y],
            dst_ref=maxima.at[y],
            send_sem=m_send.at[i],
            recv_sem=m_recv.at[i],
            device_id={"replica": (opposite, pair, next_)[i]},
            device_id_type=MESH,
        )

    for i in range(3):
        max_copy(i).start()
    weights_wait(11)
    weights_start(17)
    for i in range(3):
        max_copy(i).wait()
    largest = jnp.maximum(jnp.maximum(maxima[0], maxima[1]), jnp.maximum(maxima[2], maxima[3]))
    scales_ref[...] = largest + 1e-6

    def code(b, _):
        rows = pl.ds(pl.multiple_of(b * BLOCK, BLOCK), BLOCK)
        res[rows, :] = (corr[rows, :] / scales_ref[pl.ds(b, 1), :]).astype(BF16)
        return 0

    lax.fori_loop(0, D // BLOCK, code, 0)

    def code_copy(i):
        peer = (opposite, pair, next_)[i]
        return pltpu.make_async_remote_copy(
            src_ref=res.at[pl.ds(pl.multiple_of(peer * SHARD, SHARD), SHARD)],
            dst_ref=code_got.at[i],
            send_sem=c_send.at[i],
            recv_sem=c_recv.at[i],
            device_id={"replica": peer},
            device_id_type=MESH,
        )

    for i in range(3):
        code_copy(i).start()

    weights_wait(10, 14, 15, 16, 17)
    lax.fori_loop(0, 4, partial(1), 0)
    send_back(1, 0, 4)

    def came_back(s, _):
        give_back(s).wait()
        return 0

    def combine(g):
        rows = slice(g * 128, (g + 1) * 128)
        back_b = ret[g * 8 : g * 8 + 8, :, HALF_D:WIDE].reshape(128, SHARD)
        for q in range(2):
            columns = slice(q * SHARD, (q + 1) * SHARD)
            total = dot(pick_t[0, :, rows], ret[g * 8 : g * 8 + 8, :, columns].reshape(128, SHARD))
            total = total + dot(pick_t[1 + q, :, rows], back_b)
            if g > 0:
                total = total + total_in[:, columns]
            if g < 3:
                total_in[:, columns] = total
            else:
                grad_in_ref[:, columns] = total.astype(BF16)

    for g in range(3):
        lax.fori_loop(max(1, g * 8), g * 8 + 8, came_back, 0)
        combine(g)

    for i in range(3):
        code_copy(i).wait()

    def add_codes(t, _):
        rows = pl.ds(pl.multiple_of(t * 128, 128), 128)
        total = res[pl.ds(pl.multiple_of(y * SHARD + t * 128, 128), 128), :].astype(F32)
        for i in range(3):
            total = total + code_got[i, rows, :].astype(F32)
        sums_ref[rows, :] = total
        return 0

    lax.fori_loop(0, SHARD // 128, add_codes, 0)
    lax.fori_loop(24, EXPERTS, came_back, 0)
    combine(3)

    for number in range(18):
        weight_copy(number).wait_send()
    for stage, half in ((0, near), (1, 1 - near)):
        @pl.when(half != core)
        def _(stage=stage):
            for g in range(4):
                swap(stage, g).wait_send()


def local(grad_out, gates, expert_ids, gate_pre, up_pre, w_gate, w_up, w_down, residual):
    whole = pl.BlockSpec(memory_space=pltpu.VMEM)
    hbm = pl.BlockSpec(memory_space=pl.ANY)
    message = (EXPERTS, 16, WIDE)
    dma = pltpu.SemaphoreType.DMA
    saved = [a.reshape(EXPERTS, CAP, GROUP) for a in (gate_pre, up_pre)]
    grad_in, code_sums, scales = pl.pallas_call(
        kernel,
        out_shape=(
            jax.ShapeDtypeStruct((TOKENS, HALF_D), BF16),
            jax.ShapeDtypeStruct((SHARD, GROUP), F32),
            jax.ShapeDtypeStruct((D // BLOCK, GROUP), F32),
        ),
        in_specs=[whole, whole] + [hbm] * 7,
        out_specs=(whole, whole, whole),
        scratch_shapes=[
            pltpu.VMEM(message, BF16),
            pltpu.VMEM((2,) + message, BF16),
            pltpu.VMEM(message, BF16),
            pltpu.VMEM((2,) + message, BF16),
            pltpu.VMEM(message, BF16),
            pltpu.VMEM((3, REPLICAS, SHARD, GROUP), BF16),
            pltpu.VMEM((2, SLOTS, HALF_D), BF16),
            pltpu.VMEM((3, ROWS_A, TOKENS), BF16),
            pltpu.VMEM((3, TOKENS, ROWS_A), BF16),
            pltpu.VMEM((TOKENS, HALF_D), BF16),
            pltpu.VMEM((EXPERTS, CAP, GROUP), BF16),
            pltpu.VMEM((EXPERTS, CAP, GROUP), BF16),
            pltpu.VMEM((SLOTS, GROUP), BF16),
            pltpu.VMEM((SLOTS, GROUP), F32),
            pltpu.VMEM((SLOTS, GROUP), F32),
            pltpu.VMEM((SLOTS, GROUP), BF16),
            pltpu.VMEM((SLOTS, GROUP), BF16),
            pltpu.VMEM((D, GROUP), BF16),
            pltpu.VMEM((D, GROUP), F32),
            pltpu.VMEM((3, SHARD, GROUP), BF16),
            pltpu.VMEM((REPLICAS, D // BLOCK, GROUP), F32),
            pltpu.VMEM((TOKENS, HALF_D), F32),
            dma((EXPERTS,)),
            dma((EXPERTS,)),
            dma((EXPERTS,)),
            dma((EXPERTS,)),
            dma((EXPERTS,)),
            dma((EXPERTS,)),
            dma((18,)),
            dma((18,)),
            dma((4,)),
            dma((4,)),
            dma((3,)),
            dma((3,)),
            dma((3,)),
            dma((3,)),
            dma((8,)),
        ],
        compiler_params=pltpu.CompilerParams(
            collective_id=0, has_side_effects=True, vmem_limit_bytes=62 * 2**20
        ),
        cost_estimate=pl.CostEstimate(flops=11_300_000_000, bytes_accessed=14_000_000, transcendentals=400_000),
    )(
        expert_ids.T, gates.T, grad_out, *saved, w_gate[0], w_up[0], w_down[0], residual[0]
    )
    return grad_in, code_sums[None], scales[None]


def solution(mesh):
    spec = P("expert", "replica", "tensor")
    tokens = P(("expert", "replica"), None)
    in_specs = (tokens,) * 3 + (spec,) * 6
    out_specs = (P(("expert", "replica"), "tensor"), spec, P("expert", None, "tensor"))
    return jax.shard_map(local, mesh=mesh, in_specs=in_specs, out_specs=out_specs, check_vma=False)
```

```python
import jax
import jax.numpy as jnp
from jax import lax
from jax.experimental import pallas as pl
from jax.experimental.pallas import tpu as pltpu
from jax.sharding import PartitionSpec as P

MESH = pl.DeviceIdType.MESH
BF16, F32 = jnp.bfloat16, jnp.float32

EXPERTS, REPLICAS = 32, 4
TOKENS, TOP, CAP = 128, 4, 24
D, GROUP, SHARD, BLOCK = 3584, 512, 896, 128
HALF_D = D // 2
ROWS_A, ROWS_B = EXPERTS * 16, EXPERTS * 8
SLOTS = ROWS_A + ROWS_B
WIDE = 3 * SHARD
CUT = SHARD // 2
TILE = 8 * CAP


def dot(a, b, dims=((1,), (0,))):
    return lax.dot_general(a, b, (dims, ((), ())), preferred_element_type=F32)


def kernel(
    ids_ref, gates_ref, grad_hbm, gate_hbm, up_hbm, wg_hbm, wu_hbm, wd_hbm, res_hbm,
    grad_in_ref, sums_ref, scales_ref,
    out, rcv, ret, part, part_got, wf, routed, pick, pick_t, grad, gate_pre, up_pre,
    hid, fac_gate, fac_up, gate_grad, up_grad, res, corr, code_got, code_sum, maxima, total_in,
    a_send, a_recv, f_send, f_recv, r_send, r_recv, w_send, w_recv, p_send, p_recv,
    m_send, m_recv, c_send, c_recv, l_sem,
):
    me = lax.axis_index("expert")
    y = lax.axis_index("replica")
    core = lax.axis_index("tensor")
    other = 1 - core
    odd = lax.rem(y, 2)
    near = lax.div(y, 2)
    pair = y + 1 - 2 * odd
    next_ = lax.rem(y + 3 + 2 * odd, REPLICAS)
    opposite = lax.rem(y + 2, REPLICAS)
    weights = (wd_hbm, wg_hbm, wu_hbm)

    grad_copy = pltpu.make_async_copy(
        grad_hbm.at[:, pl.ds(pl.multiple_of(core * HALF_D, HALF_D), HALF_D)], grad, l_sem.at[0]
    )
    res_copy = pltpu.make_async_copy(res_hbm, res, l_sem.at[3])
    own_weights = [pltpu.make_async_copy(weights[w], wf.at[w, y], l_sem.at[4 + w]) for w in range(3)]
    saved = [
        pltpu.make_async_copy(gate_hbm, gate_pre, l_sem.at[1]),
        pltpu.make_async_copy(up_hbm, up_pre, l_sem.at[2]),
    ]
    for copy in [grad_copy] + saved + own_weights + [res_copy]:
        copy.start()

    barrier = pltpu.get_barrier_semaphore()

    def greet(i, _):
        pl.semaphore_signal(
            barrier, inc=1, device_id={"expert": lax.rem(me + i, EXPERTS)}, device_id_type=MESH
        )
        return 0

    for peer in (pair, next_, opposite):
        pl.semaphore_signal(barrier, inc=1, device_id={"replica": peer}, device_id_type=MESH)
    pl.semaphore_signal(barrier, inc=1, device_id={"tensor": other}, device_id_type=MESH)
    lax.fori_loop(1, EXPERTS, greet, 0)

    ids = ids_ref[...].astype(F32)
    expert_row = lax.broadcasted_iota(jnp.int32, (EXPERTS, TOKENS), 0).astype(F32)
    named = jnp.zeros((EXPERTS, TOKENS), F32)
    for k in range(TOP):
        named = named + jnp.where(ids[k : k + 1, :] == expert_row, 1.0, 0.0)
    before = jnp.where(
        lax.broadcasted_iota(jnp.int32, (TOKENS, TOKENS), 0)
        < lax.broadcasted_iota(jnp.int32, (TOKENS, TOKENS), 1),
        1.0,
        0.0,
    ).astype(BF16)
    earlier = dot(named.astype(BF16), before)
    keys = []
    for k in range(TOP):
        id_k = ids[k : k + 1, :]
        slot_k = jnp.sum(jnp.where(id_k == expert_row, earlier, 0.0), axis=0, keepdims=True)
        keys.append(id_k * 32.0 + slot_k)
    row = lax.broadcasted_iota(jnp.int32, (ROWS_A, 1), 0)
    in_row = jnp.bitwise_and(row, 15)
    base = jnp.bitwise_and(me + jnp.right_shift(row, 4), EXPERTS - 1) * 32
    key_a = (base + in_row).astype(F32)
    key_b = (base + 16 + jnp.bitwise_and(row, 7)).astype(F32)
    lower = in_row < 8
    hot = jnp.zeros((ROWS_A, TOKENS), F32)
    weigh = jnp.zeros((ROWS_A, TOKENS), F32)
    hot_b = jnp.zeros((ROWS_A, TOKENS), F32)
    weigh_b = jnp.zeros((ROWS_A, TOKENS), F32)
    for k in range(TOP):
        same = key_a == keys[k]
        same_b = key_b == keys[k]
        gate_k = gates_ref[k : k + 1, :]
        hot = hot + jnp.where(same, 1.0, 0.0)
        weigh = weigh + jnp.where(same, gate_k, 0.0)
        hot_b = hot_b + jnp.where(same_b, 1.0, 0.0)
        weigh_b = weigh_b + jnp.where(same_b, gate_k, 0.0)
    gate_a = jnp.sum(weigh, axis=1, keepdims=True)
    gate_b = jnp.sum(weigh_b, axis=1, keepdims=True)
    pick[0] = hot.astype(BF16)
    pick[1] = jnp.where(lower, hot_b, 0.0).astype(BF16)
    pick[2] = jnp.where(lower, 0.0, hot_b).astype(BF16)

    def weight_copy(number):
        if number < 12:
            w, lo = number % 6 // 2, number % 2 * CUT
            owner, peer = y, (pair if number < 6 else next_)
            src = weights[w].at[pl.ds(lo, CUT)]
        else:
            w, lo = ((0, 0), (0, CUT), (2, 0), (1, 0), (1, CUT), (2, CUT))[number - 12]
            owner, peer = (pair, next_) if number < 15 else (next_, pair)
            src = wf.at[w, owner, pl.ds(lo, CUT)]
        return pltpu.make_async_remote_copy(
            src_ref=src,
            dst_ref=wf.at[w, owner, pl.ds(lo, CUT)],
            send_sem=w_send.at[number],
            recv_sem=w_recv.at[number],
            device_id={"replica": peer},
            device_id_type=MESH,
        )

    def weights_start(*numbers):
        for number in numbers:
            weight_copy(number).start()

    def weights_wait(*numbers):
        for number in numbers:
            weight_copy(number).wait_recv()

    pl.semaphore_wait(barrier, EXPERTS + 3)
    weights_start(0, 6, 1, 7, 2, 3, 4, 5)

    def dispatch(s):
        return pltpu.make_async_remote_copy(
            src_ref=out.at[s],
            dst_ref=rcv.at[core, s],
            send_sem=a_send.at[s],
            recv_sem=a_recv.at[s],
            device_id={"expert": lax.rem(me + s, EXPERTS)},
            device_id_type=MESH,
        )

    def start_dispatch(s, _):
        dispatch(s).start()
        return 0

    grad_copy.wait()
    own = pltpu.make_async_copy(out.at[0], rcv.at[core, 0], l_sem.at[7])
    for q in range(4):
        rows = pl.ds(q * 128, 128)
        block = dot(pick[0, rows, :], grad[...]) * gate_a[q * 128 : (q + 1) * 128]
        out[pl.ds(q * 8, 8), :, 0:HALF_D] = block.astype(BF16).reshape(8, 16, HALF_D)
        block = dot(pick[1, rows, :], grad[:, 0:SHARD]) + dot(pick[2, rows, :], grad[:, SHARD:HALF_D])
        block = block * gate_b[q * 128 : (q + 1) * 128]
        out[pl.ds(q * 8, 8), :, HALF_D:WIDE] = block.astype(BF16).reshape(8, 16, SHARD)
        lax.fori_loop(max(1, q * 8), q * 8 + 8, start_dispatch, 0)
        if q == 0:
            own.start()

    def share(s):
        return pltpu.make_async_remote_copy(
            src_ref=rcv.at[core, s],
            dst_ref=rcv.at[core, s],
            send_sem=f_send.at[s],
            recv_sem=f_recv.at[s],
            device_id={"tensor": other},
            device_id_type=MESH,
        )

    def pass_on(s, _):
        dispatch(s).wait_recv()
        share(s).start()
        return 0

    def share_got(s, _):
        share(s).wait()
        return 0

    own.wait()
    share(0).start()

    for copy in saved:
        copy.wait()

    def activate(j, _):
        a, u = [], []
        for s in (2 * j, 2 * j + 1):
            source = lax.rem(me + EXPERTS - s, EXPERTS)
            a.append(gate_pre[source].astype(F32))
            u.append(up_pre[source].astype(F32))
        first = lax.div(j, 4) * TILE
        step = lax.rem(j, 4)
        for lo, hi, at in ((0, 16, first + step * 32), (16, 24, first + 128 + step * 16)):
            a_part = jnp.concatenate([v[lo:hi] for v in a], axis=0)
            u_part = jnp.concatenate([v[lo:hi] for v in u], axis=0)
            sigma = 1.0 / (1.0 + jnp.exp(-a_part))
            silu = a_part * sigma
            to = pl.ds(pl.multiple_of(at, 16), 2 * (hi - lo))
            hid[to, :] = (silu * u_part).astype(BF16)
            fac_up[to, :] = silu
            fac_gate[to, :] = u_part * sigma * (1.0 + a_part * (1.0 - sigma))
        return 0

    lax.fori_loop(0, EXPERTS // 2, activate, 0)

    def tile_of(g):
        return pl.ds(pl.multiple_of(g * TILE, TILE), TILE)

    def unfold(g):
        lax.fori_loop(g * 8, g * 8 + 8, share_got, 0)
        for h in range(2):
            routed[h, g * TILE : g * TILE + 128, :] = rcv[h, g * 8 : g * 8 + 8, :, 0:HALF_D].reshape(128, HALF_D)
            raw = rcv[h, g * 8 : g * 8 + 8, :, HALF_D:WIDE].astype(F32).reshape(8, 2, 8, SHARD)
            for q in range(2):
                routed[h, g * TILE + 128 : (g + 1) * TILE, q * SHARD : (q + 1) * SHARD] = (
                    raw[:, q].reshape(64, SHARD).astype(BF16)
                )

    def w_half(w, h):
        return wf[w, pl.ds(2 * h, 2)].reshape(HALF_D, GROUP)

    def hidden_grads(g, _):
        rows = tile_of(g)
        total = dot(routed[0, rows, :], w_half(0, 0)) + dot(routed[1, rows, :], w_half(0, 1))
        gate_grad[rows, :] = (total * fac_gate[rows, :]).astype(BF16)
        up_grad[rows, :] = (total * fac_up[rows, :]).astype(BF16)
        return 0

    def correct(lo, hi, first, last):
        for h in range(2):
            def step(t, _, h=h):
                columns = pl.ds(pl.multiple_of(t * 256, 256), 256)
                rows = pl.ds(pl.multiple_of(h * HALF_D + t * 256, 256), 256)
                total = dot(routed[h, lo:hi, columns], hid[lo:hi, :], ((0,), (0,)))
                total = total + (res[rows, :].astype(F32) if first else corr[rows, :])
                corr[rows, :] = total
                if last:
                    for b in range(2):
                        top = jnp.max(jnp.abs(total[b * BLOCK : (b + 1) * BLOCK]), axis=0, keepdims=True)
                        maxima[y, pl.ds(h * 14 + t * 2 + b, 1), :] = top
                return 0

            lax.fori_loop(0, 7, step, 0)

    def swap(stage, g):
        block = pl.ds(g * 8, 8)
        return pltpu.make_async_remote_copy(
            src_ref=part.at[stage, block],
            dst_ref=part_got.at[block],
            send_sem=p_send.at[g],
            recv_sem=p_recv.at[g],
            device_id={"tensor": other},
            device_id_type=MESH,
        )

    def partial(stage):
        half = near if stage == 0 else 1 - near

        def group(g, _):
            rows = tile_of(g)
            values = []
            for q in range(2):
                s = 2 * half + q
                value = dot(gate_grad[rows, :], wf[1, s], ((1,), (1,))) + dot(
                    up_grad[rows, :], wf[2, s], ((1,), (1,))
                )
                part[stage, pl.ds(g * 8, 8), :, q * SHARD : (q + 1) * SHARD] = (
                    value[0:128].astype(BF16).reshape(8, 16, SHARD)
                )
                values.append(value[128:TILE].reshape(8, 1, 8, SHARD))
            both = jnp.concatenate(values, axis=1).reshape(8, 16, SHARD)
            part[stage, pl.ds(g * 8, 8), :, HALF_D:WIDE] = both.astype(BF16)

            @pl.when(half != core)
            def _():
                swap(stage, g).start()

            return 0

        return group

    def give_back(s):
        return pltpu.make_async_remote_copy(
            src_ref=out.at[s],
            dst_ref=ret.at[s],
            send_sem=r_send.at[s],
            recv_sem=r_recv.at[s],
            device_id={"expert": lax.rem(me + EXPERTS - s, EXPERTS)},
            device_id_type=MESH,
        )

    def send_back(stage, lo, hi):
        half = near if stage == 0 else 1 - near

        def summed(s):
            return (part[stage, s].astype(F32) + part_got[s].astype(F32)).astype(BF16)

        def one(s, _):
            dispatch(s).wait_send()
            out[s] = summed(s)
            give_back(s).start()
            return 0

        @pl.when(half == core)
        def _():
            for g in range(lo, hi):
                swap(stage, g).wait_recv()
                if g == 0:
                    ret[0] = summed(0)
                lax.fori_loop(max(1, g * 8), g * 8 + 8, one, 0)

    lax.fori_loop(1, 3, pass_on, 0)
    weights_wait(0)
    weights_start(12)
    lax.fori_loop(3, 6, pass_on, 0)
    weights_wait(1)
    weights_start(13, 8, 9, 11, 10)
    for j in range(3):
        pick_t[j] = jnp.transpose(pick[j].astype(F32)).astype(BF16)
    lax.fori_loop(6, 8, pass_on, 0)
    unfold(0)
    lax.fori_loop(8, 16, pass_on, 0)
    unfold(1)
    own_weights[0].wait()
    weights_wait(6, 7, 12, 13)
    lax.fori_loop(0, 2, hidden_grads, 0)
    res_copy.wait()
    correct(0, 2 * TILE, True, False)
    lax.fori_loop(16, 24, pass_on, 0)
    unfold(2)
    hidden_grads(2, 0)
    weights_wait(8, 4)
    weights_start(15, 14)
    lax.fori_loop(24, 28, pass_on, 0)
    own_weights[1].wait()
    own_weights[2].wait()
    weights_wait(2, 3, 5)
    lax.fori_loop(0, 2, partial(0), 0)
    lax.fori_loop(28, EXPERTS, pass_on, 0)
    partial(0)(2, 0)
    weights_wait(9)
    weights_start(16)
    send_back(0, 0, 3)
    unfold(3)
    hidden_grads(3, 0)
    partial(0)(3, 0)
    send_back(0, 3, 4)
    weights_wait(11)
    weights_start(17)
    correct(2 * TILE, SLOTS, False, True)

    def max_copy(i):
        return pltpu.make_async_remote_copy(
            src_ref=maxima.at[y],
            dst_ref=maxima.at[y],
            send_sem=m_send.at[i],
            recv_sem=m_recv.at[i],
            device_id={"replica": (opposite, pair, next_)[i]},
            device_id_type=MESH,
        )

    for i in range(3):
        max_copy(i).start()
    for i in range(3):
        max_copy(i).wait()
    largest = jnp.maximum(jnp.maximum(maxima[0], maxima[1]), jnp.maximum(maxima[2], maxima[3]))
    scales_ref[...] = largest + 1e-6

    def code(b, _):
        rows = pl.ds(pl.multiple_of(b * BLOCK, BLOCK), BLOCK)
        res[rows, :] = (corr[rows, :] / scales_ref[pl.ds(b, 1), :]).astype(BF16)
        return 0

    lax.fori_loop(0, D // BLOCK, code, 0)

    def code_rows(owner, lo):
        return pl.ds(pl.multiple_of(owner * SHARD + lo, CUT), CUT)

    def code_copy(i):
        peer = (pair, next_, pair, next_, pair, next_)[i]
        owner = (opposite, opposite, pair, next_, pair, next_)[i]
        lo = (CUT, 0, CUT, 0, 0, CUT)[i]
        src = res.at[code_rows(owner, lo)] if i < 4 else code_sum.at[i - 4]
        return pltpu.make_async_remote_copy(
            src_ref=src,
            dst_ref=code_got.at[i],
            send_sem=c_send.at[i],
            recv_sem=c_recv.at[i],
            device_id={"replica": peer},
            device_id_type=MESH,
        )

    for i in range(4):
        code_copy(i).start()

    def code_pass(i):
        code_copy(1 - i).wait_recv()
        owner, lo = ((pair, 0), (next_, CUT))[i]
        code_sum[i] = (res[code_rows(owner, lo), :].astype(F32) + code_got[1 - i].astype(F32)).astype(BF16)
        code_copy(4 + i).start()

    weights_wait(10, 14, 15, 16, 17)
    lax.fori_loop(0, 4, partial(1), 0)
    send_back(1, 0, 4)
    for i in range(2):
        code_pass(i)

    def came_back(s, _):
        give_back(s).wait()
        return 0

    def combine(g):
        rows = slice(g * 128, (g + 1) * 128)
        back_b = ret[g * 8 : g * 8 + 8, :, HALF_D:WIDE].reshape(128, SHARD)
        for q in range(2):
            columns = slice(q * SHARD, (q + 1) * SHARD)
            total = dot(pick_t[0, :, rows], ret[g * 8 : g * 8 + 8, :, columns].reshape(128, SHARD))
            total = total + dot(pick_t[1 + q, :, rows], back_b)
            if g > 0:
                total = total + total_in[:, columns]
            if g < 3:
                total_in[:, columns] = total
            else:
                grad_in_ref[:, columns] = total.astype(BF16)

    for g in range(3):
        lax.fori_loop(max(1, g * 8), g * 8 + 8, came_back, 0)
        combine(g)

    for i in range(2, 6):
        code_copy(i).wait_recv()

    def add_codes(t, _):
        rows = pl.ds(pl.multiple_of(t * 64, 64), 64)
        for lo, first, second in ((0, 3, 4), (CUT, 2, 5)):
            total = res[pl.ds(pl.multiple_of(y * SHARD + lo + t * 64, 64), 64), :].astype(F32)
            for i in (first, second):
                total = total + code_got[i, rows, :].astype(F32)
            sums_ref[pl.ds(pl.multiple_of(lo + t * 64, 64), 64), :] = total
        return 0

    lax.fori_loop(0, CUT // 64, add_codes, 0)
    lax.fori_loop(24, EXPERTS, came_back, 0)
    combine(3)

    for number in range(18):
        weight_copy(number).wait_send()
    for i in range(6):
        code_copy(i).wait_send()
    for stage, half in ((0, near), (1, 1 - near)):
        @pl.when(half != core)
        def _(stage=stage):
            for g in range(4):
                swap(stage, g).wait_send()


def hand_out(grad_ref, sums_ref, scales_ref, grad_out, sums_out, scales_out, sem):
    copies = [
        pltpu.make_async_copy(grad_ref, grad_out, sem.at[0]),
        pltpu.make_async_copy(sums_ref, sums_out, sem.at[1]),
    ]
    for copy in copies:
        copy.start()
    for b in range(D // BLOCK):
        scales_out[b] = scales_ref[b : b + 1, :]
    for copy in copies:
        copy.wait()


def local(grad_out, gates, expert_ids, gate_pre, up_pre, w_gate, w_up, w_down, residual):
    whole = pl.BlockSpec(memory_space=pltpu.VMEM)
    hbm = pl.BlockSpec(memory_space=pl.ANY)
    message = (EXPERTS, 16, WIDE)
    dma = pltpu.SemaphoreType.DMA
    saved = [a.reshape(EXPERTS, CAP, GROUP) for a in (gate_pre, up_pre)]
    grad_in, code_sums, scales = pl.pallas_call(
        kernel,
        out_shape=(
            jax.ShapeDtypeStruct((TOKENS, HALF_D), BF16),
            jax.ShapeDtypeStruct((SHARD, GROUP), F32),
            jax.ShapeDtypeStruct((D // BLOCK, GROUP), F32),
        ),
        in_specs=[whole, whole] + [hbm] * 7,
        out_specs=(whole, whole, whole),
        scratch_shapes=[
            pltpu.VMEM(message, BF16),
            pltpu.VMEM((2,) + message, BF16),
            pltpu.VMEM(message, BF16),
            pltpu.VMEM((2,) + message, BF16),
            pltpu.VMEM(message, BF16),
            pltpu.VMEM((3, REPLICAS, SHARD, GROUP), BF16),
            pltpu.VMEM((2, SLOTS, HALF_D), BF16),
            pltpu.VMEM((3, ROWS_A, TOKENS), BF16),
            pltpu.VMEM((3, TOKENS, ROWS_A), BF16),
            pltpu.VMEM((TOKENS, HALF_D), BF16),
            pltpu.VMEM((EXPERTS, CAP, GROUP), BF16),
            pltpu.VMEM((EXPERTS, CAP, GROUP), BF16),
            pltpu.VMEM((SLOTS, GROUP), BF16),
            pltpu.VMEM((SLOTS, GROUP), F32),
            pltpu.VMEM((SLOTS, GROUP), F32),
            pltpu.VMEM((SLOTS, GROUP), BF16),
            pltpu.VMEM((SLOTS, GROUP), BF16),
            pltpu.VMEM((D, GROUP), BF16),
            pltpu.VMEM((D, GROUP), F32),
            pltpu.VMEM((6, CUT, GROUP), BF16),
            pltpu.VMEM((2, CUT, GROUP), BF16),
            pltpu.VMEM((REPLICAS, D // BLOCK, GROUP), F32),
            pltpu.VMEM((TOKENS, HALF_D), F32),
            dma((EXPERTS,)),
            dma((EXPERTS,)),
            dma((EXPERTS,)),
            dma((EXPERTS,)),
            dma((EXPERTS,)),
            dma((EXPERTS,)),
            dma((18,)),
            dma((18,)),
            dma((4,)),
            dma((4,)),
            dma((3,)),
            dma((3,)),
            dma((6,)),
            dma((6,)),
            dma((8,)),
        ],
        compiler_params=pltpu.CompilerParams(
            collective_id=0, has_side_effects=True, vmem_limit_bytes=62 * 2**20
        ),
        cost_estimate=pl.CostEstimate(flops=11_300_000_000, bytes_accessed=14_000_000, transcendentals=400_000),
    )(
        expert_ids.T, gates.T, grad_out, *saved, w_gate[0], w_up[0], w_down[0], residual[0]
    )
    grad_in, code_sums, scales = pl.pallas_call(
        hand_out,
        out_shape=(
            jax.ShapeDtypeStruct((TOKENS, HALF_D), BF16),
            jax.ShapeDtypeStruct((SHARD, GROUP), F32),
            jax.ShapeDtypeStruct((D // BLOCK, 1, GROUP), F32),
        ),
        in_specs=[whole] * 3,
        out_specs=(hbm, hbm, whole),
        scratch_shapes=[dma((2,))],
    )(grad_in, code_sums, scales)
    return grad_in, code_sums[None], scales.reshape(1, D // BLOCK, GROUP)


def solution(mesh):
    spec = P("expert", "replica", "tensor")
    tokens = P(("expert", "replica"), None)
    in_specs = (tokens,) * 3 + (spec,) * 6
    out_specs = (P(("expert", "replica"), "tensor"), spec, P("expert", None, "tensor"))
    return jax.shard_map(local, mesh=mesh, in_specs=in_specs, out_specs=out_specs, check_vma=False)
```

```python
import jax
import jax.numpy as jnp
from jax import lax
from jax.experimental import pallas as pl
from jax.experimental.pallas import tpu as pltpu
from jax.sharding import PartitionSpec as P

MESH = pl.DeviceIdType.MESH
BF16, F32 = jnp.bfloat16, jnp.float32

EXPERTS, REPLICAS, RING = 32, 4, 8
TOKENS, TOP, CAP = 128, 4, 24
D, GROUP, SHARD, BLOCK = 3584, 512, 896, 128
HALF_D = D // 2
ROWS_A, ROWS_B = EXPERTS * 16, EXPERTS * 8
SLOTS = ROWS_A + ROWS_B
WIDE = 3 * SHARD
CUT = SHARD // 2
TILE = 8 * CAP


def dot(a, b, dims=((1,), (0,))):
    return lax.dot_general(a, b, (dims, ((), ())), preferred_element_type=F32)


def kernel(
    ids_ref, gates_ref, grad_hbm, gate_hbm, up_hbm, wg_hbm, wu_hbm, wd_hbm, res_hbm,
    grad_in_ref, sums_ref, scales_ref,
    out, rcv, ret, part, part_got, wf, routed, pick, pick_t, info, grad, gate_pre, up_pre,
    hid, fac_gate, fac_up, gate_grad, up_grad, res, corr, code_sum, maxima, total_in,
    g_send, g_recv, i_send, i_recv,
    a_send, a_recv, f_send, f_recv, r_send, r_recv, w_send, w_recv, p_send, p_recv,
    m_send, m_recv, c_send, c_recv, l_sem,
):
    me = lax.axis_index("expert")
    y = lax.axis_index("replica")
    core = lax.axis_index("tensor")
    other = 1 - core
    odd = lax.rem(y, 2)
    near = lax.div(y, 2)
    pair = y + 1 - 2 * odd
    next_ = lax.rem(y + 3 + 2 * odd, REPLICAS)
    opposite = lax.rem(y + 2, REPLICAS)
    weights = (wd_hbm, wg_hbm, wu_hbm)

    x, z = lax.div(me, RING), lax.rem(me, RING)

    def turn(k):
        return lax.div(k + 1, 2) * (1 - 2 * lax.rem(k, 2))

    def place(x_, z_):
        return lax.rem(x_ + 4, 4) * RING + lax.rem(z_ + RING, RING)

    def source(s):
        return place(x - lax.rem(s, 4), z + turn(lax.div(s, 4)))

    grad_copy = pltpu.make_async_copy(
        grad_hbm.at[:, pl.ds(pl.multiple_of(core * HALF_D, HALF_D), HALF_D)], grad.at[0], l_sem.at[0]
    )
    res_copy = pltpu.make_async_copy(res_hbm, res, l_sem.at[3])
    own_weights = [pltpu.make_async_copy(weights[w], wf.at[w, y], l_sem.at[4 + w]) for w in range(3)]
    saved = [
        pltpu.make_async_copy(gate_hbm, gate_pre, l_sem.at[1]),
        pltpu.make_async_copy(up_hbm, up_pre, l_sem.at[2]),
    ]
    for copy in [grad_copy] + saved + own_weights + [res_copy]:
        copy.start()

    barrier = pltpu.get_barrier_semaphore()

    def greet(i, _):
        pl.semaphore_signal(
            barrier, inc=1, device_id={"expert": lax.rem(me + i, EXPERTS)}, device_id_type=MESH
        )
        return 0

    for peer in (pair, next_, opposite):
        pl.semaphore_signal(barrier, inc=1, device_id={"replica": peer}, device_id_type=MESH)
    pl.semaphore_signal(barrier, inc=1, device_id={"tensor": other}, device_id_type=MESH)
    lax.fori_loop(1, EXPERTS, greet, 0)

    ids = ids_ref[...].astype(F32)
    expert_row = lax.broadcasted_iota(jnp.int32, (EXPERTS, TOKENS), 0).astype(F32)
    named = jnp.zeros((EXPERTS, TOKENS), F32)
    for k in range(TOP):
        named = named + jnp.where(ids[k : k + 1, :] == expert_row, 1.0, 0.0)
    before = jnp.where(
        lax.broadcasted_iota(jnp.int32, (TOKENS, TOKENS), 0)
        < lax.broadcasted_iota(jnp.int32, (TOKENS, TOKENS), 1),
        1.0,
        0.0,
    ).astype(BF16)
    earlier = dot(named.astype(BF16), before)
    for k in range(TOP):
        id_k = ids[k : k + 1, :]
        slot_k = jnp.sum(jnp.where(id_k == expert_row, earlier, 0.0), axis=0, keepdims=True)
        info[0, k : k + 1, :] = id_k * 32.0 + slot_k
    info[0, TOP : 2 * TOP, :] = gates_ref[...]

    def ring_copy(way, r):
        chain = ((0, 1, 3, 5, 7), (0, 2, 4, 6, 7))[way]
        hop, lo = r // 2, (r % 2 if way == 0 else 1 - r % 2) * 64
        return pltpu.make_async_remote_copy(
            src_ref=grad.at[chain[hop], pl.ds(lo, 64)],
            dst_ref=grad.at[chain[hop + 1], pl.ds(lo, 64)],
            send_sem=g_send.at[way * 7 + r],
            recv_sem=g_recv.at[way * 7 + r],
            device_id={"expert": place(x, z + 1 - 2 * way)},
            device_id_type=MESH,
        )

    def ring_step(r):
        for way in range(2):
            ring_copy(way, r).wait_recv()
            if r + 2 <= 6:
                ring_copy(way, r + 2).start()

    def info_copy(k):
        return pltpu.make_async_remote_copy(
            src_ref=info.at[0],
            dst_ref=info.at[k],
            send_sem=i_send.at[k],
            recv_sem=i_recv.at[k],
            device_id={"expert": place(x, z - turn(k))},
            device_id_type=MESH,
        )

    def weight_copy(number):
        if number < 12:
            w, lo = number % 6 // 2, number % 2 * CUT
            owner, peer = y, (pair if number < 6 else next_)
            src = weights[w].at[pl.ds(lo, CUT)]
        else:
            w, lo = ((0, 0), (0, CUT), (2, 0), (1, 0), (1, CUT), (2, CUT))[number - 12]
            owner, peer = (pair, next_) if number < 15 else (next_, pair)
            src = wf.at[w, owner, pl.ds(lo, CUT)]
        return pltpu.make_async_remote_copy(
            src_ref=src,
            dst_ref=wf.at[w, owner, pl.ds(lo, CUT)],
            send_sem=w_send.at[number],
            recv_sem=w_recv.at[number],
            device_id={"replica": peer},
            device_id_type=MESH,
        )

    def weights_start(*numbers):
        for number in numbers:
            weight_copy(number).start()

    def weights_wait(*numbers):
        for number in numbers:
            weight_copy(number).wait_recv()

    pl.semaphore_wait(barrier, EXPERTS + 3)
    weights_start(0, 6, 1, 7, 2, 3, 4, 5)

    for k in range(1, RING):
        info_copy(k).start()
    grad_copy.wait()
    for r in range(2):
        for way in range(2):
            ring_copy(way, r).start()

    def dispatch(s):
        return pltpu.make_async_remote_copy(
            src_ref=out.at[s],
            dst_ref=rcv.at[core, s],
            send_sem=a_send.at[s],
            recv_sem=a_recv.at[s],
            device_id={"expert": place(x + lax.rem(s, 4), z)},
            device_id_type=MESH,
        )

    def share(k):
        block = rcv.at[core, pl.ds(4 * k, 4)]
        return pltpu.make_async_remote_copy(
            src_ref=block,
            dst_ref=block,
            send_sem=f_send.at[k],
            recv_sem=f_recv.at[k],
            device_id={"tensor": other},
            device_id_type=MESH,
        )

    def pass_on(g):
        for k in (2 * g, 2 * g + 1):
            for j in range(1, 4):
                dispatch(4 * k + j).wait_recv()
            share(k).start()

    def send_block(k):
        if k > 0:
            info_copy(k).wait_recv()
        row = lax.broadcasted_iota(jnp.int32, (64, 1), 0)
        in_row = jnp.bitwise_and(row, 15)
        base = (jnp.bitwise_and(x + jnp.right_shift(row, 4), 3) * RING + z) * 32
        key_a = (base + in_row).astype(F32)
        key_b = (base + 16 + jnp.bitwise_and(row, 7)).astype(F32)
        hot = weigh = hot_b = weigh_b = jnp.zeros((64, TOKENS), F32)
        for p in range(TOP):
            same = key_a == info[k, p : p + 1, :]
            same_b = key_b == info[k, p : p + 1, :]
            gate = info[k, TOP + p : TOP + p + 1, :]
            hot = hot + jnp.where(same, 1.0, 0.0)
            weigh = weigh + jnp.where(same, gate, 0.0)
            hot_b = hot_b + jnp.where(same_b, 1.0, 0.0)
            weigh_b = weigh_b + jnp.where(same_b, gate, 0.0)
        gate_a = jnp.sum(weigh, axis=1, keepdims=True)
        gate_b = jnp.sum(weigh_b, axis=1, keepdims=True)
        low = jnp.concatenate([hot, jnp.where(in_row < 8, hot_b, 0.0)], axis=0).astype(BF16)
        high = jnp.concatenate([hot, jnp.where(in_row < 8, 0.0, hot_b)], axis=0).astype(BF16)
        left = dot(low, grad[k, :, 0:SHARD])
        right = dot(high, grad[k, :, SHARD:HALF_D])
        rows = (
            (left[0:64] * gate_a, 0),
            (right[0:64] * gate_a, SHARD),
            ((left[64:128] + right[64:128]) * gate_b, HALF_D),
        )
        for value, at in rows:
            value = value.astype(BF16).reshape(4, 16, SHARD)
            rcv[core, 4 * k, :, at : at + SHARD] = value[0]
            out[4 * k + 1 : 4 * k + 4, :, at : at + SHARD] = value[1:4]
        for j in range(1, 4):
            dispatch(4 * k + j).start()

    send_block(0)

    for copy in saved:
        copy.wait()

    def activate(j, _):
        a, u = [], []
        for s in (2 * j, 2 * j + 1):
            block = source(s)
            a.append(gate_pre[block].astype(F32))
            u.append(up_pre[block].astype(F32))
        first = lax.div(j, 4) * TILE
        step = lax.rem(j, 4)
        for lo, hi, at in ((0, 16, first + step * 32), (16, 24, first + 128 + step * 16)):
            a_part = jnp.concatenate([v[lo:hi] for v in a], axis=0)
            u_part = jnp.concatenate([v[lo:hi] for v in u], axis=0)
            sigma = 1.0 / (1.0 + jnp.exp(-a_part))
            silu = a_part * sigma
            to = pl.ds(pl.multiple_of(at, 16), 2 * (hi - lo))
            hid[to, :] = (silu * u_part).astype(BF16)
            fac_up[to, :] = silu
            fac_gate[to, :] = u_part * sigma * (1.0 + a_part * (1.0 - sigma))
        return 0

    lax.fori_loop(0, EXPERTS // 2, activate, 0)

    def tile_of(g):
        return pl.ds(pl.multiple_of(g * TILE, TILE), TILE)

    def unfold(g):
        for k in (2 * g, 2 * g + 1):
            share(k).wait()
        for h in range(2):
            routed[h, g * TILE : g * TILE + 128, :] = rcv[h, g * 8 : g * 8 + 8, :, 0:HALF_D].reshape(128, HALF_D)
            raw = rcv[h, g * 8 : g * 8 + 8, :, HALF_D:WIDE].astype(F32).reshape(8, 2, 8, SHARD)
            for q in range(2):
                routed[h, g * TILE + 128 : (g + 1) * TILE, q * SHARD : (q + 1) * SHARD] = (
                    raw[:, q].reshape(64, SHARD).astype(BF16)
                )

    def w_half(w, h):
        return wf[w, pl.ds(2 * h, 2)].reshape(HALF_D, GROUP)

    def hidden_grads(g, _):
        rows = tile_of(g)
        total = dot(routed[0, rows, :], w_half(0, 0)) + dot(routed[1, rows, :], w_half(0, 1))
        by_gate = (total * fac_gate[rows, :]).astype(BF16)
        by_up = (total * fac_up[rows, :]).astype(BF16)
        for lo, hi, to in ((0, 128, g * 128), (128, TILE, ROWS_A + g * 64)):
            to = pl.ds(pl.multiple_of(to, 64), hi - lo)
            gate_grad[to, :] = by_gate[lo:hi]
            up_grad[to, :] = by_up[lo:hi]
        return 0

    def correct(lo, hi, first, last, halves):
        for h in halves:
            def step(t, _, h=h):
                columns = pl.ds(pl.multiple_of(t * 256, 256), 256)
                rows = pl.ds(pl.multiple_of(h * HALF_D + t * 256, 256), 256)
                total = dot(routed[h, lo:hi, columns], hid[lo:hi, :], ((0,), (0,)))
                total = total + (res[rows, :].astype(F32) if first else corr[rows, :])
                corr[rows, :] = total
                if last:
                    for b in range(2):
                        top = jnp.max(jnp.abs(total[b * BLOCK : (b + 1) * BLOCK]), axis=0, keepdims=True)
                        maxima[y, pl.ds(h * 14 + t * 2 + b, 1), :] = top
                return 0

            lax.fori_loop(0, 7, step, 0)

    SPANS = ((0, SHARD), (SHARD, WIDE))

    def half_of(stage):
        return near if stage == 0 else 1 - near

    def swap(stage, phase, g):
        lo, hi = SPANS[phase]
        block = (pl.ds(g * 8, 8), slice(None), slice(lo, hi))
        return pltpu.make_async_remote_copy(
            src_ref=part.at[(stage,) + block],
            dst_ref=part_got.at[block],
            send_sem=p_send.at[phase * 4 + g],
            recv_sem=p_recv.at[phase * 4 + g],
            device_id={"tensor": other},
            device_id_type=MESH,
        )

    def partial(stage, phase):
        shards = ((y, pair), (next_, opposite))[stage]

        for lo in range(0, SHARD, 256):
            hi = min(lo + 256, SHARD)

            def value(rows, s, lo=lo, hi=hi):
                return dot(gate_grad[rows, :], wf[1, s, lo:hi, :], ((1,), (1,))) + dot(
                    up_grad[rows, :], wf[2, s, lo:hi, :], ((1,), (1,))
                )

            at = phase * SHARD + lo
            part[stage, :, :, at : at + hi - lo] = (
                value(slice(0, ROWS_A), shards[phase]).astype(BF16).reshape(EXPERTS, 16, hi - lo)
            )
            if phase == 1:
                both = [value(slice(ROWS_A, SLOTS), s).reshape(EXPERTS, 1, 8, hi - lo) for s in shards]
                both = jnp.concatenate(both, axis=1).reshape(EXPERTS, 16, hi - lo)
                part[stage, :, :, HALF_D + lo : HALF_D + hi] = both.astype(BF16)

        @pl.when(half_of(stage) != core)
        def _():
            for g in range(4):
                swap(stage, phase, g).start()

    def give_back(phase, s):
        lo, hi = SPANS[phase]
        return pltpu.make_async_remote_copy(
            src_ref=out.at[s, :, lo:hi],
            dst_ref=ret.at[s, :, lo:hi],
            send_sem=r_send.at[phase * EXPERTS + s],
            recv_sem=r_recv.at[phase * EXPERTS + s],
            device_id={"expert": source(s)},
            device_id_type=MESH,
        )

    def send_back(stage, phase):
        lo, hi = SPANS[phase]

        def summed(s):
            return (part[stage, s, :, lo:hi].astype(F32) + part_got[s, :, lo:hi].astype(F32)).astype(BF16)

        def one(s, _):
            out[s, :, lo:hi] = summed(s)
            give_back(phase, s).start()
            return 0

        @pl.when(half_of(stage) == core)
        def _():
            for g in range(4):
                swap(stage, phase, g).wait_recv()
                if g == 0:
                    ret[0, :, lo:hi] = summed(0)
                lax.fori_loop(max(1, g * 8), g * 8 + 8, one, 0)

    ring_step(0)
    ring_step(1)
    weights_wait(0)
    weights_start(12)
    send_block(1)
    send_block(2)
    ring_step(2)
    ring_step(3)
    weights_wait(1)
    weights_start(13, 8, 9)
    send_block(3)
    send_block(4)
    pass_on(0)
    ring_step(4)
    unfold(0)
    ring_step(5)
    send_block(5)
    send_block(6)
    pass_on(1)
    unfold(1)
    res_copy.wait()
    correct(0, 2 * TILE, True, False, (0,))
    ring_step(6)
    send_block(7)
    pass_on(2)
    unfold(2)
    pass_on(3)
    correct(0, 2 * TILE, True, False, (1,))
    unfold(3)
    own_weights[0].wait()
    weights_wait(6, 7, 12, 13)
    lax.fori_loop(0, 4, hidden_grads, 0)
    own_weights[1].wait()
    own_weights[2].wait()
    partial(0, 0)
    weights_start(11)

    def dispatched(i, _):
        dispatch(lax.div(i, 3) * 4 + 1 + lax.rem(i, 3)).wait_send()
        return 0

    lax.fori_loop(0, 24, dispatched, 0)
    send_back(0, 0)
    weights_wait(8, 4)
    weights_start(15)
    correct(2 * TILE, SLOTS, False, True, (0, 1))
    for number in (12, 13):
        weight_copy(number).wait_send()

    def max_copy(i):
        return pltpu.make_async_remote_copy(
            src_ref=maxima.at[y],
            dst_ref=maxima.at[y],
            send_sem=m_send.at[i],
            recv_sem=m_recv.at[i],
            device_id={"replica": (opposite, pair, next_)[i]},
            device_id_type=MESH,
        )

    for i in range(3):
        max_copy(i).start()
    weights_start(10, 14)
    weights_wait(2, 3, 5)
    weights_wait(9)
    weights_start(16)
    partial(0, 1)
    send_back(0, 1)

    row = lax.broadcasted_iota(jnp.int32, (ROWS_A, 1), 0)
    in_row = jnp.bitwise_and(row, 15)
    ring = jnp.right_shift(row, 6)
    turned = jnp.right_shift(ring + 1, 1) * (1 - 2 * jnp.bitwise_and(ring, 1))
    expert = jnp.bitwise_and(x + jnp.right_shift(row, 4), 3) * RING + jnp.bitwise_and(z - turned, RING - 1)
    key_a = (expert * 32 + in_row).astype(F32)
    key_b = (expert * 32 + 16 + jnp.bitwise_and(row, 7)).astype(F32)
    hot = hot_b = jnp.zeros((ROWS_A, TOKENS), F32)
    for p in range(TOP):
        hot = hot + jnp.where(key_a == info[0, p : p + 1, :], 1.0, 0.0)
        hot_b = hot_b + jnp.where(key_b == info[0, p : p + 1, :], 1.0, 0.0)
    pick[0] = hot
    pick[1] = jnp.where(in_row < 8, hot_b, 0.0)
    pick[2] = jnp.where(in_row < 8, 0.0, hot_b)
    for j in range(3):
        pick_t[j] = jnp.transpose(pick[j]).astype(BF16)

    weights_wait(11)
    weights_start(17)
    for i in range(3):
        max_copy(i).wait()
    largest = jnp.maximum(jnp.maximum(maxima[0], maxima[1]), jnp.maximum(maxima[2], maxima[3]))
    scales_ref[...] = largest + 1e-6

    def code(b, _):
        rows = pl.ds(pl.multiple_of(b * BLOCK, BLOCK), BLOCK)
        res[rows, :] = (corr[rows, :] / scales_ref[pl.ds(b, 1), :]).astype(BF16)
        return 0

    lax.fori_loop(0, D // BLOCK, code, 0)

    def code_rows(owner, lo):
        return pl.ds(pl.multiple_of(owner * SHARD + lo, CUT), CUT)

    def code_got(i):
        return wf.at[0, i // 2, pl.ds(i % 2 * CUT, CUT)]

    def code_copy(i):
        peer = (pair, next_, pair, next_, pair, next_)[i]
        owner = (opposite, opposite, pair, next_, pair, next_)[i]
        lo = (CUT, 0, CUT, 0, 0, CUT)[i]
        src = res.at[code_rows(owner, lo)] if i < 4 else code_sum.at[i - 4]
        return pltpu.make_async_remote_copy(
            src_ref=src,
            dst_ref=code_got(i),
            send_sem=c_send.at[i],
            recv_sem=c_recv.at[i],
            device_id={"replica": peer},
            device_id_type=MESH,
        )

    for i in range(4):
        code_copy(i).start()

    def code_pass(i):
        code_copy(1 - i).wait_recv()
        owner, lo = ((pair, 0), (next_, CUT))[i]
        code_sum[i] = (res[code_rows(owner, lo), :].astype(F32) + code_got(1 - i)[...].astype(F32)).astype(BF16)
        code_copy(4 + i).start()

    weights_wait(10)
    partial(1, 0)
    send_back(1, 0)
    weights_wait(14, 15, 16, 17)
    partial(1, 1)
    send_back(1, 1)
    for i in range(2):
        code_pass(i)

    def came_back(s, _):
        give_back(0, s).wait()
        give_back(1, s).wait()
        return 0

    def combine(g):
        rows = slice(g * 128, (g + 1) * 128)
        back_b = ret[g * 8 : g * 8 + 8, :, HALF_D:WIDE].reshape(128, SHARD)
        for q in range(2):
            columns = slice(q * SHARD, (q + 1) * SHARD)
            total = dot(pick_t[0, :, rows], ret[g * 8 : g * 8 + 8, :, columns].reshape(128, SHARD))
            total = total + dot(pick_t[1 + q, :, rows], back_b)
            if g > 0:
                total = total + total_in[:, columns]
            if g < 3:
                total_in[:, columns] = total
            else:
                shard = jnp.where(core == near, (y, pair)[q], (next_, opposite)[q])
                to = pl.ds(pl.multiple_of(lax.rem(shard, 2) * SHARD, SHARD), SHARD)
                grad_in_ref[:, to] = total.astype(BF16)

    for g in range(3):
        lax.fori_loop(max(1, g * 8), g * 8 + 8, came_back, 0)
        combine(g)

    for i in range(2, 6):
        code_copy(i).wait_recv()

    def add_codes(t, _):
        rows = pl.ds(pl.multiple_of(t * 64, 64), 64)
        for lo, first, second in ((0, 3, 4), (CUT, 2, 5)):
            total = res[pl.ds(pl.multiple_of(y * SHARD + lo + t * 64, 64), 64), :].astype(F32)
            for i in (first, second):
                total = total + wf[0, i // 2, pl.ds(pl.multiple_of(i % 2 * CUT + t * 64, 64), 64), :].astype(F32)
            sums_ref[pl.ds(pl.multiple_of(lo + t * 64, 64), 64), :] = total
        return 0

    lax.fori_loop(0, CUT // 64, add_codes, 0)
    lax.fori_loop(24, EXPERTS, came_back, 0)
    combine(3)

    for number in range(18):
        if number not in (12, 13):
            weight_copy(number).wait_send()
    for k in range(1, RING):
        info_copy(k).wait_send()
    for r in range(7):
        for way in range(2):
            ring_copy(way, r).wait_send()
    for i in range(6):
        code_copy(i).wait_send()
    for stage, half in ((0, near), (1, 1 - near)):
        @pl.when(half != core)
        def _(stage=stage):
            for g in range(4):
                for phase in range(2):
                    swap(stage, phase, g).wait_send()


def hand_out(grad_ref, sums_ref, scales_ref, grad_out, sums_out, scales_out, sem):
    copies = [
        pltpu.make_async_copy(grad_ref, grad_out, sem.at[0]),
        pltpu.make_async_copy(sums_ref, sums_out, sem.at[1]),
    ]
    for copy in copies:
        copy.start()
    for b in range(D // BLOCK):
        scales_out[b] = scales_ref[b : b + 1, :]
    for copy in copies:
        copy.wait()


def local(grad_out, gates, expert_ids, gate_pre, up_pre, w_gate, w_up, w_down, residual):
    whole = pl.BlockSpec(memory_space=pltpu.VMEM)
    hbm = pl.BlockSpec(memory_space=pl.ANY)
    message = (EXPERTS, 16, WIDE)
    dma = pltpu.SemaphoreType.DMA
    saved = [a.reshape(EXPERTS, CAP, GROUP) for a in (gate_pre, up_pre)]
    grad_in, code_sums, scales = pl.pallas_call(
        kernel,
        out_shape=(
            jax.ShapeDtypeStruct((TOKENS, HALF_D), BF16),
            jax.ShapeDtypeStruct((SHARD, GROUP), F32),
            jax.ShapeDtypeStruct((D // BLOCK, GROUP), F32),
        ),
        in_specs=[whole, whole] + [hbm] * 7,
        out_specs=(whole, whole, whole),
        scratch_shapes=[
            pltpu.VMEM(message, BF16),
            pltpu.VMEM((2,) + message, BF16),
            pltpu.VMEM(message, BF16),
            pltpu.VMEM((2,) + message, BF16),
            pltpu.VMEM(message, BF16),
            pltpu.VMEM((3, REPLICAS, SHARD, GROUP), BF16),
            pltpu.VMEM((2, SLOTS, HALF_D), BF16),
            pltpu.VMEM((3, ROWS_A, TOKENS), F32),
            pltpu.VMEM((3, TOKENS, ROWS_A), BF16),
            pltpu.VMEM((RING, 2 * TOP, TOKENS), F32),
            pltpu.VMEM((RING, TOKENS, HALF_D), BF16),
            pltpu.VMEM((EXPERTS, CAP, GROUP), BF16),
            pltpu.VMEM((EXPERTS, CAP, GROUP), BF16),
            pltpu.VMEM((SLOTS, GROUP), BF16),
            pltpu.VMEM((SLOTS, GROUP), F32),
            pltpu.VMEM((SLOTS, GROUP), F32),
            pltpu.VMEM((SLOTS, GROUP), BF16),
            pltpu.VMEM((SLOTS, GROUP), BF16),
            pltpu.VMEM((D, GROUP), BF16),
            pltpu.VMEM((D, GROUP), F32),
            pltpu.VMEM((2, CUT, GROUP), BF16),
            pltpu.VMEM((REPLICAS, D // BLOCK, GROUP), F32),
            pltpu.VMEM((TOKENS, HALF_D), F32),
            dma((14,)),
            dma((14,)),
            dma((RING,)),
            dma((RING,)),
            dma((EXPERTS,)),
            dma((EXPERTS,)),
            dma((EXPERTS,)),
            dma((EXPERTS,)),
            dma((2 * EXPERTS,)),
            dma((2 * EXPERTS,)),
            dma((18,)),
            dma((18,)),
            dma((8,)),
            dma((8,)),
            dma((3,)),
            dma((3,)),
            dma((6,)),
            dma((6,)),
            dma((8,)),
        ],
        compiler_params=pltpu.CompilerParams(
            collective_id=0, has_side_effects=True, vmem_limit_bytes=62 * 2**20
        ),
        cost_estimate=pl.CostEstimate(flops=11_300_000_000, bytes_accessed=14_000_000, transcendentals=400_000),
    )(
        expert_ids.T, gates.T, grad_out, *saved, w_gate[0], w_up[0], w_down[0], residual[0]
    )
    grad_in, code_sums, scales = pl.pallas_call(
        hand_out,
        out_shape=(
            jax.ShapeDtypeStruct((TOKENS, HALF_D), BF16),
            jax.ShapeDtypeStruct((SHARD, GROUP), F32),
            jax.ShapeDtypeStruct((D // BLOCK, 1, GROUP), F32),
        ),
        in_specs=[whole] * 3,
        out_specs=(hbm, hbm, whole),
        scratch_shapes=[dma((2,))],
    )(grad_in, code_sums, scales)
    return grad_in, code_sums[None], scales.reshape(1, D // BLOCK, GROUP)


def solution(mesh):
    spec = P("expert", "replica", "tensor")
    tokens = P(("expert", "replica"), None)
    in_specs = (tokens,) * 3 + (spec,) * 6
    out_specs = (P(("expert", "replica"), "tensor"), spec, P("expert", None, "tensor"))
    return jax.shard_map(local, mesh=mesh, in_specs=in_specs, out_specs=out_specs, check_vma=False)
```

```python
import jax
import jax.numpy as jnp
from jax import lax
from jax.experimental import pallas as pl
from jax.experimental.pallas import tpu as pltpu
from jax.sharding import PartitionSpec as P

MESH = pl.DeviceIdType.MESH
BF16, F32 = jnp.bfloat16, jnp.float32

EXPERTS, REPLICAS, RING = 32, 4, 8
TOKENS, TOP, CAP = 128, 4, 24
D, GROUP, SHARD, BLOCK = 3584, 512, 896, 128
HALF_D = D // 2
ROWS_A, ROWS_B = EXPERTS * 16, EXPERTS * 8
SLOTS = ROWS_A + ROWS_B
WIDE = 3 * SHARD
CUT = SHARD // 2
TILE = 8 * CAP


def dot(a, b, dims=((1,), (0,))):
    return lax.dot_general(a, b, (dims, ((), ())), preferred_element_type=F32)


def kernel(
    ids_ref, gates_ref, grad_hbm, gate_hbm, up_hbm, wg_hbm, wu_hbm, wd_hbm, res_hbm,
    grad_in_hbm, sums_hbm, scales_hbm,
    grad_in_ref, sums_ref, scales_ref, out, rcv, ret, part, part_got, wf, routed, pick, pick_t, info, grad, gate_pre, up_pre,
    hid, fac_gate, fac_up, gate_grad, up_grad, res, corr, code_sum, own_max, maxima, total_in,
    g_send, g_recv, i_send, i_recv,
    a_send, a_recv, f_send, f_recv, r_send, r_recv, w_send, w_recv, p_send, p_recv,
    m_send, m_recv, c_send, c_recv, l_sem,
):
    me = lax.axis_index("expert")
    y = lax.axis_index("replica")
    core = lax.axis_index("tensor")
    other = 1 - core
    odd = lax.rem(y, 2)
    near = lax.div(y, 2)
    pair = y + 1 - 2 * odd
    next_ = lax.rem(y + 3 + 2 * odd, REPLICAS)
    opposite = lax.rem(y + 2, REPLICAS)
    weights = (wd_hbm, wg_hbm, wu_hbm)

    x, z = lax.div(me, RING), lax.rem(me, RING)

    def turn(k):
        return lax.div(k + 1, 2) * (1 - 2 * lax.rem(k, 2))

    def place(x_, z_):
        return lax.rem(x_ + 4, 4) * RING + lax.rem(z_ + RING, RING)

    def source(s):
        return place(x - lax.rem(s, 4), z + turn(lax.div(s, 4)))

    grad_copy = pltpu.make_async_copy(
        grad_hbm.at[:, pl.ds(pl.multiple_of(core * HALF_D, HALF_D), HALF_D)], grad.at[0], l_sem.at[0]
    )
    res_copy = pltpu.make_async_copy(res_hbm, res, l_sem.at[3])
    own_weights = [pltpu.make_async_copy(weights[w], wf.at[w, y], l_sem.at[4 + w]) for w in range(3)]
    saved = [
        pltpu.make_async_copy(gate_hbm, gate_pre, l_sem.at[1]),
        pltpu.make_async_copy(up_hbm, up_pre, l_sem.at[2]),
    ]
    barrier = pltpu.get_barrier_semaphore()

    def greet(i, _):
        pl.semaphore_signal(
            barrier, inc=1, device_id={"expert": lax.rem(me + i, EXPERTS)}, device_id_type=MESH
        )
        return 0

    for peer in (pair, next_, opposite):
        pl.semaphore_signal(barrier, inc=1, device_id={"replica": peer}, device_id_type=MESH)
    pl.semaphore_signal(barrier, inc=1, device_id={"tensor": other}, device_id_type=MESH)
    lax.fori_loop(1, EXPERTS, greet, 0)
    for copy in [grad_copy] + saved + own_weights + [res_copy]:
        copy.start()

    def weight_copy(number):
        if number < 12:
            w, lo = number % 6 // 2, number % 2 * CUT
            owner, peer = y, (pair if number < 6 else next_)
            src = weights[w].at[pl.ds(lo, CUT)]
        else:
            w, lo = ((0, 0), (0, CUT), (2, 0), (1, 0), (1, CUT), (2, CUT))[number - 12]
            owner, peer = (pair, next_) if number < 15 else (next_, pair)
            src = wf.at[w, owner, pl.ds(lo, CUT)]
        return pltpu.make_async_remote_copy(
            src_ref=src,
            dst_ref=wf.at[w, owner, pl.ds(lo, CUT)],
            send_sem=w_send.at[number],
            recv_sem=w_recv.at[number],
            device_id={"replica": peer},
            device_id_type=MESH,
        )

    def weights_start(*numbers):
        for number in numbers:
            weight_copy(number).start()

    def weights_wait(*numbers):
        for number in numbers:
            weight_copy(number).wait_recv()


    pl.semaphore_wait(barrier, EXPERTS + 3)
    weights_start(0, 6, 1, 7, 2, 3, 4, 5)

    ids = ids_ref[...].astype(F32)
    expert_row = lax.broadcasted_iota(jnp.int32, (EXPERTS, TOKENS), 0).astype(F32)
    named = jnp.zeros((EXPERTS, TOKENS), F32)
    for k in range(TOP):
        named = named + jnp.where(ids[k : k + 1, :] == expert_row, 1.0, 0.0)
    before = jnp.where(
        lax.broadcasted_iota(jnp.int32, (TOKENS, TOKENS), 0)
        < lax.broadcasted_iota(jnp.int32, (TOKENS, TOKENS), 1),
        1.0,
        0.0,
    ).astype(BF16)
    earlier = dot(named.astype(BF16), before)
    for k in range(TOP):
        id_k = ids[k : k + 1, :]
        slot_k = jnp.sum(jnp.where(id_k == expert_row, earlier, 0.0), axis=0, keepdims=True)
        info[0, k : k + 1, :] = id_k * 32.0 + slot_k
    info[0, TOP : 2 * TOP, :] = gates_ref[...]

    def ring_copy(way, r):
        chain = ((0, 1, 3, 5, 7), (0, 2, 4, 6, 7))[way]
        hop, lo = r // 2, (r % 2 if way == 0 else 1 - r % 2) * 64
        return pltpu.make_async_remote_copy(
            src_ref=grad.at[chain[hop], pl.ds(lo, 64)],
            dst_ref=grad.at[chain[hop + 1], pl.ds(lo, 64)],
            send_sem=g_send.at[way * 7 + r],
            recv_sem=g_recv.at[way * 7 + r],
            device_id={"expert": place(x, z + 1 - 2 * way)},
            device_id_type=MESH,
        )

    def ring_step(r):
        for way in range(2):
            ring_copy(way, r).wait_recv()
            if r + 2 <= 6:
                ring_copy(way, r + 2).start()

    def info_copy(k):
        return pltpu.make_async_remote_copy(
            src_ref=info.at[0],
            dst_ref=info.at[k],
            send_sem=i_send.at[k],
            recv_sem=i_recv.at[k],
            device_id={"expert": place(x, z - turn(k))},
            device_id_type=MESH,
        )

    for k in range(1, RING):
        info_copy(k).start()
    grad_copy.wait()
    for r in range(2):
        for way in range(2):
            ring_copy(way, r).start()

    def dispatch(s):
        return pltpu.make_async_remote_copy(
            src_ref=out.at[s],
            dst_ref=rcv.at[core, s],
            send_sem=a_send.at[s],
            recv_sem=a_recv.at[s],
            device_id={"expert": place(x + lax.rem(s, 4), z)},
            device_id_type=MESH,
        )

    def share(k):
        block = rcv.at[core, pl.ds(4 * k, 4)]
        return pltpu.make_async_remote_copy(
            src_ref=block,
            dst_ref=block,
            send_sem=f_send.at[k],
            recv_sem=f_recv.at[k],
            device_id={"tensor": other},
            device_id_type=MESH,
        )

    def pass_on(g):
        for k in (2 * g, 2 * g + 1):
            for j in range(1, 4):
                dispatch(4 * k + j).wait_recv()
            share(k).start()

    def send_block(k):
        if k > 0:
            info_copy(k).wait_recv()
        row = lax.broadcasted_iota(jnp.int32, (64, 1), 0)
        in_row = jnp.bitwise_and(row, 15)
        base = (jnp.bitwise_and(x + jnp.right_shift(row, 4), 3) * RING + z) * 32
        key_a = (base + in_row).astype(F32)
        key_b = (base + 16 + jnp.bitwise_and(row, 7)).astype(F32)
        hot = weigh = hot_b = weigh_b = jnp.zeros((64, TOKENS), F32)
        for p in range(TOP):
            same = key_a == info[k, p : p + 1, :]
            same_b = key_b == info[k, p : p + 1, :]
            gate = info[k, TOP + p : TOP + p + 1, :]
            hot = hot + jnp.where(same, 1.0, 0.0)
            weigh = weigh + jnp.where(same, gate, 0.0)
            hot_b = hot_b + jnp.where(same_b, 1.0, 0.0)
            weigh_b = weigh_b + jnp.where(same_b, gate, 0.0)
        gate_a = jnp.sum(weigh, axis=1, keepdims=True)
        gate_b = jnp.sum(weigh_b, axis=1, keepdims=True)
        low = jnp.concatenate([hot, jnp.where(in_row < 8, hot_b, 0.0)], axis=0).astype(BF16)
        high = jnp.concatenate([hot, jnp.where(in_row < 8, 0.0, hot_b)], axis=0).astype(BF16)
        left = dot(low, grad[k, :, 0:SHARD])
        right = dot(high, grad[k, :, SHARD:HALF_D])
        rows = (
            (left[0:64] * gate_a, 0),
            (right[0:64] * gate_a, SHARD),
            ((left[64:128] + right[64:128]) * gate_b, HALF_D),
        )
        for value, at in rows:
            value = value.astype(BF16).reshape(4, 16, SHARD)
            rcv[core, 4 * k, :, at : at + SHARD] = value[0]
            out[4 * k + 1 : 4 * k + 4, :, at : at + SHARD] = value[1:4]
        for j in range(1, 4):
            dispatch(4 * k + j).start()

    send_block(0)

    for copy in saved:
        copy.wait()

    def activate(j, _):
        a, u = [], []
        for s in (2 * j, 2 * j + 1):
            block = source(s)
            a.append(gate_pre[block].astype(F32))
            u.append(up_pre[block].astype(F32))
        first = lax.div(j, 4) * TILE
        step = lax.rem(j, 4)
        for lo, hi, at in ((0, 16, first + step * 32), (16, 24, first + 128 + step * 16)):
            a_part = jnp.concatenate([v[lo:hi] for v in a], axis=0)
            u_part = jnp.concatenate([v[lo:hi] for v in u], axis=0)
            sigma = 1.0 / (1.0 + jnp.exp(-a_part))
            silu = a_part * sigma
            to = pl.ds(pl.multiple_of(at, 16), 2 * (hi - lo))
            hid[to, :] = (silu * u_part).astype(BF16)
            fac_up[to, :] = silu
            fac_gate[to, :] = u_part * sigma * (1.0 + a_part * (1.0 - sigma))
        return 0

    lax.fori_loop(0, EXPERTS // 2, activate, 0)

    def tile_of(g):
        return pl.ds(pl.multiple_of(g * TILE, TILE), TILE)

    def unfold(g):
        for k in (2 * g, 2 * g + 1):
            share(k).wait()
        for h in range(2):
            routed[h, g * TILE : g * TILE + 128, :] = rcv[h, g * 8 : g * 8 + 8, :, 0:HALF_D].reshape(128, HALF_D)
            raw = rcv[h, g * 8 : g * 8 + 8, :, HALF_D:WIDE].astype(F32).reshape(8, 2, 8, SHARD)
            for q in range(2):
                routed[h, g * TILE + 128 : (g + 1) * TILE, q * SHARD : (q + 1) * SHARD] = (
                    raw[:, q].reshape(64, SHARD).astype(BF16)
                )

    def w_half(w, h):
        return wf[w, pl.ds(2 * h, 2)].reshape(HALF_D, GROUP)

    def hidden_grads(g, _):
        rows = tile_of(g)
        total = dot(routed[0, rows, :], w_half(0, 0)) + dot(routed[1, rows, :], w_half(0, 1))
        by_gate = (total * fac_gate[rows, :]).astype(BF16)
        by_up = (total * fac_up[rows, :]).astype(BF16)
        for lo, hi, to in ((0, 128, g * 128), (128, TILE, ROWS_A + g * 64)):
            to = pl.ds(pl.multiple_of(to, 64), hi - lo)
            gate_grad[to, :] = by_gate[lo:hi]
            up_grad[to, :] = by_up[lo:hi]
        return 0

    def correct(lo, hi, first, last, halves):
        for h in halves:
            def step(t, _, h=h):
                columns = pl.ds(pl.multiple_of(t * 256, 256), 256)
                rows = pl.ds(pl.multiple_of(h * HALF_D + t * 256, 256), 256)
                total = dot(routed[h, lo:hi, columns], hid[lo:hi, :], ((0,), (0,)))
                total = total + (res[rows, :].astype(F32) if first else corr[rows, :])
                corr[rows, :] = total
                if last:
                    for b in range(2):
                        top = jnp.max(jnp.abs(total[b * BLOCK : (b + 1) * BLOCK]), axis=0, keepdims=True)
                        own_max[pl.ds(h * 14 + t * 2 + b, 1), :] = top
                return 0

            lax.fori_loop(0, 7, step, 0)

    SPANS = ((0, SHARD), (SHARD, WIDE))

    def half_of(stage):
        return near if stage == 0 else 1 - near

    def swap(stage, phase, g):
        lo, hi = SPANS[phase]
        block = (pl.ds(g * 8, 8), slice(None), slice(lo, hi))
        return pltpu.make_async_remote_copy(
            src_ref=part.at[(stage,) + block],
            dst_ref=part_got.at[block],
            send_sem=p_send.at[phase * 4 + g],
            recv_sem=p_recv.at[phase * 4 + g],
            device_id={"tensor": other},
            device_id_type=MESH,
        )

    def partial(stage, phase):
        shards = ((y, pair), (next_, opposite))[stage]

        for lo in range(0, SHARD, 256):
            hi = min(lo + 256, SHARD)

            def value(rows, s, lo=lo, hi=hi):
                return dot(gate_grad[rows, :], wf[1, s, lo:hi, :], ((1,), (1,))) + dot(
                    up_grad[rows, :], wf[2, s, lo:hi, :], ((1,), (1,))
                )

            at = phase * SHARD + lo
            part[stage, :, :, at : at + hi - lo] = (
                value(slice(0, ROWS_A), shards[phase]).astype(BF16).reshape(EXPERTS, 16, hi - lo)
            )
            if phase == 1:
                both = [value(slice(ROWS_A, SLOTS), s).reshape(EXPERTS, 1, 8, hi - lo) for s in shards]
                both = jnp.concatenate(both, axis=1).reshape(EXPERTS, 16, hi - lo)
                part[stage, :, :, HALF_D + lo : HALF_D + hi] = both.astype(BF16)

        @pl.when(half_of(stage) != core)
        def _():
            for g in range(4):
                swap(stage, phase, g).start()

    def give_back(phase, s):
        lo, hi = SPANS[phase]
        return pltpu.make_async_remote_copy(
            src_ref=out.at[s, :, lo:hi],
            dst_ref=ret.at[s, :, lo:hi],
            send_sem=r_send.at[phase * EXPERTS + s],
            recv_sem=r_recv.at[phase * EXPERTS + s],
            device_id={"expert": source(s)},
            device_id_type=MESH,
        )

    def send_back(stage, phase):
        lo, hi = SPANS[phase]

        def summed(s):
            return (part[stage, s, :, lo:hi].astype(F32) + part_got[s, :, lo:hi].astype(F32)).astype(BF16)

        def one(s, _):
            out[s, :, lo:hi] = summed(s)
            give_back(phase, s).start()
            return 0

        @pl.when(half_of(stage) == core)
        def _():
            for g in range(4):
                swap(stage, phase, g).wait_recv()
                if g == 0:
                    ret[0, :, lo:hi] = summed(0)
                lax.fori_loop(max(1, g * 8), g * 8 + 8, one, 0)

    ring_step(0)
    ring_step(1)
    weights_wait(0)
    weights_start(12)
    send_block(1)
    send_block(2)
    ring_step(2)
    ring_step(3)
    weights_wait(1)
    weights_start(13, 8, 9)
    send_block(3)
    send_block(4)
    pass_on(0)
    ring_step(4)
    unfold(0)
    ring_step(5)
    send_block(5)
    send_block(6)
    pass_on(1)
    unfold(1)
    res_copy.wait()
    correct(0, 2 * TILE, True, False, (0,))
    ring_step(6)
    send_block(7)
    pass_on(2)
    unfold(2)
    pass_on(3)
    correct(0, 2 * TILE, True, False, (1,))
    unfold(3)
    own_weights[0].wait()
    weights_wait(6, 7, 12, 13)
    lax.fori_loop(0, 4, hidden_grads, 0)
    own_weights[1].wait()
    own_weights[2].wait()
    partial(0, 0)
    weights_start(11)

    def dispatched(i, _):
        dispatch(lax.div(i, 3) * 4 + 1 + lax.rem(i, 3)).wait_send()
        return 0

    lax.fori_loop(0, 24, dispatched, 0)
    send_back(0, 0)
    weights_wait(8, 4)
    weights_start(15)
    correct(2 * TILE, SLOTS, False, True, (0, 1))
    for number in (12, 13):
        weight_copy(number).wait_send()

    own_max[D // BLOCK :, :] = jnp.zeros((32 - D // BLOCK, GROUP), F32)
    maxima[y] = own_max[...].astype(BF16)

    def max_copy(i):
        return pltpu.make_async_remote_copy(
            src_ref=maxima.at[y],
            dst_ref=maxima.at[y],
            send_sem=m_send.at[i],
            recv_sem=m_recv.at[i],
            device_id={"replica": (opposite, pair, next_)[i]},
            device_id_type=MESH,
        )

    for i in range(3):
        max_copy(i).start()
    weights_start(10, 14)
    weights_wait(2, 3, 5)
    weights_wait(9)
    weights_start(16)
    partial(0, 1)
    send_back(0, 1)

    row = lax.broadcasted_iota(jnp.int32, (ROWS_A, 1), 0)
    in_row = jnp.bitwise_and(row, 15)
    ring = jnp.right_shift(row, 6)
    turned = jnp.right_shift(ring + 1, 1) * (1 - 2 * jnp.bitwise_and(ring, 1))
    expert = jnp.bitwise_and(x + jnp.right_shift(row, 4), 3) * RING + jnp.bitwise_and(z - turned, RING - 1)
    key_a = (expert * 32 + in_row).astype(F32)
    key_b = (expert * 32 + 16 + jnp.bitwise_and(row, 7)).astype(F32)
    hot = hot_b = jnp.zeros((ROWS_A, TOKENS), F32)
    for p in range(TOP):
        hot = hot + jnp.where(key_a == info[0, p : p + 1, :], 1.0, 0.0)
        hot_b = hot_b + jnp.where(key_b == info[0, p : p + 1, :], 1.0, 0.0)
    pick[0] = hot
    pick[1] = jnp.where(in_row < 8, hot_b, 0.0)
    pick[2] = jnp.where(in_row < 8, 0.0, hot_b)
    for j in range(3):
        pick_t[j] = jnp.transpose(pick[j]).astype(BF16)

    weights_wait(11)
    weights_start(17)
    for i in range(3):
        max_copy(i).wait()
    largest = maxima[0].astype(F32)
    for r in range(1, REPLICAS):
        largest = jnp.maximum(largest, maxima[r].astype(F32))
    scales_ref[...] = largest[0 : D // BLOCK] + 1e-6
    results = [pltpu.make_async_copy(scales_ref, scales_hbm, l_sem.at[7])]
    results[0].start()

    def code(b, _):
        rows = pl.ds(pl.multiple_of(b * BLOCK, BLOCK), BLOCK)
        res[rows, :] = (corr[rows, :] / scales_ref[pl.ds(b, 1), :]).astype(BF16)
        return 0

    lax.fori_loop(0, D // BLOCK, code, 0)

    def code_rows(owner, lo):
        return pl.ds(pl.multiple_of(owner * SHARD + lo, CUT), CUT)

    def code_got(i):
        return wf.at[0, i // 2, pl.ds(i % 2 * CUT, CUT)]

    def code_copy(i):
        peer = (pair, next_, pair, next_, pair, next_)[i]
        owner = (opposite, opposite, pair, next_, pair, next_)[i]
        lo = (CUT, 0, CUT, 0, 0, CUT)[i]
        src = res.at[code_rows(owner, lo)] if i < 4 else code_sum.at[i - 4]
        return pltpu.make_async_remote_copy(
            src_ref=src,
            dst_ref=code_got(i),
            send_sem=c_send.at[i],
            recv_sem=c_recv.at[i],
            device_id={"replica": peer},
            device_id_type=MESH,
        )

    for i in range(4):
        code_copy(i).start()

    def code_pass(i):
        code_copy(1 - i).wait_recv()
        owner, lo = ((pair, 0), (next_, CUT))[i]
        code_sum[i] = (res[code_rows(owner, lo), :].astype(F32) + code_got(1 - i)[...].astype(F32)).astype(BF16)
        code_copy(4 + i).start()

    weights_wait(10)
    partial(1, 0)
    send_back(1, 0)
    weights_wait(14, 15, 16, 17)
    partial(1, 1)
    send_back(1, 1)
    for i in range(2):
        code_pass(i)

    def came_back(s, _):
        give_back(0, s).wait()
        give_back(1, s).wait()
        return 0

    def combine(g):
        rows = slice(g * 128, (g + 1) * 128)
        back_b = ret[g * 8 : g * 8 + 8, :, HALF_D:WIDE].reshape(128, SHARD)
        for q in range(2):
            columns = slice(q * SHARD, (q + 1) * SHARD)
            total = dot(pick_t[0, :, rows], ret[g * 8 : g * 8 + 8, :, columns].reshape(128, SHARD))
            total = total + dot(pick_t[1 + q, :, rows], back_b)
            if g > 0:
                total = total + total_in[:, columns]
            if g < 3:
                total_in[:, columns] = total
            else:
                shard = jnp.where(core == near, (y, pair)[q], (next_, opposite)[q])
                to = pl.ds(pl.multiple_of(lax.rem(shard, 2) * SHARD, SHARD), SHARD)
                grad_in_ref[:, to] = total.astype(BF16)

    for g in range(3):
        lax.fori_loop(max(1, g * 8), g * 8 + 8, came_back, 0)
        combine(g)

    lax.fori_loop(24, EXPERTS, came_back, 0)
    combine(3)
    results.append(pltpu.make_async_copy(grad_in_ref, grad_in_hbm, l_sem.at[8]))
    results[1].start()

    for lo, first, second in ((0, 3, 4), (CUT, 2, 5)):
        code_copy(first).wait_recv()
        code_copy(second).wait_recv()

        def add_codes(t, _, lo=lo, first=first, second=second):
            rows = pl.ds(pl.multiple_of(lo + t * 64, 64), 64)
            total = res[pl.ds(pl.multiple_of(y * SHARD + lo + t * 64, 64), 64), :].astype(F32)
            for i in (first, second):
                got = pl.ds(pl.multiple_of(i % 2 * CUT + t * 64, 64), 64)
                total = total + wf[0, i // 2, got, :].astype(F32)
            sums_ref[rows, :] = total
            return 0

        lax.fori_loop(0, CUT // 64, add_codes, 0)
        rows = pl.ds(lo, CUT)
        results.append(pltpu.make_async_copy(sums_ref.at[rows], sums_hbm.at[rows], l_sem.at[9 + lo // CUT]))
        results[-1].start()

    for number in range(18):
        if number not in (12, 13):
            weight_copy(number).wait_send()
    for k in range(1, RING):
        info_copy(k).wait_send()
    for r in range(7):
        for way in range(2):
            ring_copy(way, r).wait_send()
    for i in range(6):
        code_copy(i).wait_send()
    for stage, half in ((0, near), (1, 1 - near)):
        @pl.when(half != core)
        def _(stage=stage):
            for g in range(4):
                for phase in range(2):
                    swap(stage, phase, g).wait_send()
    for copy in results:
        copy.wait()


def hand_out(grad_ref, sums_ref, scales_ref, grad_out, sums_out, scales_out, grad, sums, scales, flat, come, go):
    half = SHARD // 2
    pieces = [(scales_ref, scales, flat, scales_out), (grad_ref, grad, grad, grad_out)]
    for t in range(2):
        rows = pl.ds(t * half, half)
        pieces.append((sums_ref.at[rows], sums.at[rows], sums.at[rows], sums_out.at[rows]))
    into = [pltpu.make_async_copy(p[0], p[1], come.at[i]) for i, p in enumerate(pieces)]
    away = [pltpu.make_async_copy(p[2], p[3], go.at[i]) for i, p in enumerate(pieces)]
    for copy in into:
        copy.start()
    into[0].wait()
    for b in range(D // BLOCK):
        flat[b] = scales[b : b + 1, :]
    away[0].start()
    for first, second in zip(into[1:], away[1:]):
        first.wait()
        second.start()
    for copy in away:
        copy.wait()


def local(grad_out, gates, expert_ids, gate_pre, up_pre, w_gate, w_up, w_down, residual):
    whole = pl.BlockSpec(memory_space=pltpu.VMEM)
    hbm = pl.BlockSpec(memory_space=pl.ANY)
    message = (EXPERTS, 16, WIDE)
    dma = pltpu.SemaphoreType.DMA
    saved = [a.reshape(EXPERTS, CAP, GROUP) for a in (gate_pre, up_pre)]
    grad_in, code_sums, scales = pl.pallas_call(
        kernel,
        out_shape=(
            jax.ShapeDtypeStruct((TOKENS, HALF_D), BF16),
            jax.ShapeDtypeStruct((SHARD, GROUP), F32),
            jax.ShapeDtypeStruct((D // BLOCK, GROUP), F32),
        ),
        in_specs=[whole, whole] + [hbm] * 7,
        out_specs=(hbm, hbm, hbm),
        scratch_shapes=[
            pltpu.VMEM((TOKENS, HALF_D), BF16),
            pltpu.VMEM((SHARD, GROUP), F32),
            pltpu.VMEM((D // BLOCK, GROUP), F32),
            pltpu.VMEM(message, BF16),
            pltpu.VMEM((2,) + message, BF16),
            pltpu.VMEM(message, BF16),
            pltpu.VMEM((2,) + message, BF16),
            pltpu.VMEM(message, BF16),
            pltpu.VMEM((3, REPLICAS, SHARD, GROUP), BF16),
            pltpu.VMEM((2, SLOTS, HALF_D), BF16),
            pltpu.VMEM((3, ROWS_A, TOKENS), F32),
            pltpu.VMEM((3, TOKENS, ROWS_A), BF16),
            pltpu.VMEM((RING, 2 * TOP, TOKENS), F32),
            pltpu.VMEM((RING, TOKENS, HALF_D), BF16),
            pltpu.VMEM((EXPERTS, CAP, GROUP), BF16),
            pltpu.VMEM((EXPERTS, CAP, GROUP), BF16),
            pltpu.VMEM((SLOTS, GROUP), BF16),
            pltpu.VMEM((SLOTS, GROUP), F32),
            pltpu.VMEM((SLOTS, GROUP), F32),
            pltpu.VMEM((SLOTS, GROUP), BF16),
            pltpu.VMEM((SLOTS, GROUP), BF16),
            pltpu.VMEM((D, GROUP), BF16),
            pltpu.VMEM((D, GROUP), F32),
            pltpu.VMEM((2, CUT, GROUP), BF16),
            pltpu.VMEM((32, GROUP), F32),
            pltpu.VMEM((REPLICAS, 32, GROUP), BF16),
            pltpu.VMEM((TOKENS, HALF_D), F32),
            dma((14,)),
            dma((14,)),
            dma((RING,)),
            dma((RING,)),
            dma((EXPERTS,)),
            dma((EXPERTS,)),
            dma((EXPERTS,)),
            dma((EXPERTS,)),
            dma((2 * EXPERTS,)),
            dma((2 * EXPERTS,)),
            dma((18,)),
            dma((18,)),
            dma((8,)),
            dma((8,)),
            dma((3,)),
            dma((3,)),
            dma((6,)),
            dma((6,)),
            dma((11,)),
        ],
        compiler_params=pltpu.CompilerParams(
            collective_id=0, has_side_effects=True, vmem_limit_bytes=62 * 2**20
        ),
        cost_estimate=pl.CostEstimate(flops=11_300_000_000, bytes_accessed=14_000_000, transcendentals=400_000),
    )(
        expert_ids.T, gates.T, grad_out, *saved, w_gate[0], w_up[0], w_down[0], residual[0]
    )
    grad_in, code_sums, scales = pl.pallas_call(
        hand_out,
        out_shape=(
            jax.ShapeDtypeStruct((TOKENS, HALF_D), BF16),
            jax.ShapeDtypeStruct((SHARD, GROUP), F32),
            jax.ShapeDtypeStruct((D // BLOCK, 1, GROUP), F32),
        ),
        in_specs=[hbm, hbm, hbm],
        out_specs=(hbm, hbm, hbm),
        scratch_shapes=[
            pltpu.VMEM((TOKENS, HALF_D), BF16),
            pltpu.VMEM((SHARD, GROUP), F32),
            pltpu.VMEM((D // BLOCK, GROUP), F32),
            pltpu.VMEM((D // BLOCK, 1, GROUP), F32),
            dma((4,)),
            dma((4,)),
        ],
        compiler_params=pltpu.CompilerParams(vmem_limit_bytes=60 * 2**20),
    )(grad_in, code_sums, scales)
    return grad_in, code_sums[None], scales.reshape(1, D // BLOCK, GROUP)


def solution(mesh):
    spec = P("expert", "replica", "tensor")
    tokens = P(("expert", "replica"), None)
    in_specs = (tokens,) * 3 + (spec,) * 6
    out_specs = (P(("expert", "replica"), "tensor"), spec, P("expert", None, "tensor"))
    return jax.shard_map(local, mesh=mesh, in_specs=in_specs, out_specs=out_specs, check_vma=False)
```

```python
import jax
import jax.numpy as jnp
from jax import lax
from jax.experimental import pallas as pl
from jax.experimental.pallas import tpu as pltpu
from jax.sharding import PartitionSpec as P

MESH = pl.DeviceIdType.MESH
BF16, F32 = jnp.bfloat16, jnp.float32

EXPERTS, REPLICAS, RING = 32, 4, 8
TOKENS, TOP, CAP = 128, 4, 24
D, GROUP, SHARD, BLOCK = 3584, 512, 896, 128
HALF_D = D // 2
ROWS_A, ROWS_B = EXPERTS * 16, EXPERTS * 8
SLOTS = ROWS_A + ROWS_B
WIDE = 3 * SHARD
CUT = SHARD // 2
TILE = 8 * CAP


def dot(a, b, dims=((1,), (0,))):
    return lax.dot_general(a, b, (dims, ((), ())), preferred_element_type=F32)


def kernel(
    ids_ref, gates_ref, grad_hbm, gate_hbm, up_hbm, wg_hbm, wu_hbm, wd_hbm, res_hbm,
    grad_in_hbm, sums_hbm, scales_hbm,
    grad_in_ref, sums_ref, scales_ref, out, rcv, ret, part, part_got, wf, routed, pick, pick_t, info, grad, gate_pre, up_pre,
    hid, fac_gate, fac_up, gate_grad, up_grad, res, corr, code_sum, own_max, maxima, total_in,
    g_send, g_recv, i_send, i_recv,
    a_send, a_recv, f_send, f_recv, r_send, r_recv, w_send, w_recv, p_send, p_recv,
    m_send, m_recv, c_send, c_recv, l_sem,
):
    me = lax.axis_index("expert")
    y = lax.axis_index("replica")
    core = lax.axis_index("tensor")
    other = 1 - core
    odd = lax.rem(y, 2)
    near = lax.div(y, 2)
    pair = y + 1 - 2 * odd
    next_ = lax.rem(y + 3 + 2 * odd, REPLICAS)
    opposite = lax.rem(y + 2, REPLICAS)
    weights = (wd_hbm, wg_hbm, wu_hbm)

    x, z = lax.div(me, RING), lax.rem(me, RING)

    def turn(k):
        return lax.div(k + 1, 2) * (1 - 2 * lax.rem(k, 2))

    def place(x_, z_):
        return lax.rem(x_ + 4, 4) * RING + lax.rem(z_ + RING, RING)

    def source(s):
        return place(x - lax.rem(s, 4), z + turn(lax.div(s, 4)))

    grad_copy = pltpu.make_async_copy(
        grad_hbm.at[:, pl.ds(pl.multiple_of(core * HALF_D, HALF_D), HALF_D)], grad.at[0], l_sem.at[0]
    )
    res_copy = pltpu.make_async_copy(res_hbm, res, l_sem.at[3])
    own_weights = [pltpu.make_async_copy(weights[w], wf.at[w, y], l_sem.at[4 + w]) for w in range(3)]
    saved = [
        pltpu.make_async_copy(gate_hbm, gate_pre, l_sem.at[1]),
        pltpu.make_async_copy(up_hbm, up_pre, l_sem.at[2]),
    ]
    barrier = pltpu.get_barrier_semaphore()

    def greet(i, _):
        pl.semaphore_signal(
            barrier, inc=1, device_id={"expert": lax.rem(me + i, EXPERTS)}, device_id_type=MESH
        )
        return 0

    for peer in (pair, next_, opposite):
        pl.semaphore_signal(barrier, inc=1, device_id={"replica": peer}, device_id_type=MESH)
    pl.semaphore_signal(barrier, inc=1, device_id={"tensor": other}, device_id_type=MESH)
    lax.fori_loop(1, EXPERTS, greet, 0)
    grad_copy.start()
    def weight_copy(number):
        if number < 12:
            w, lo = number % 6 // 2, number % 2 * CUT
            owner, peer = y, (pair if number < 6 else next_)
            src = weights[w].at[pl.ds(lo, CUT)]
        else:
            w, lo = ((0, 0), (0, CUT), (2, 0), (1, 0), (1, CUT), (2, CUT))[number - 12]
            owner, peer = (pair, next_) if number < 15 else (next_, pair)
            src = wf.at[w, owner, pl.ds(lo, CUT)]
        return pltpu.make_async_remote_copy(
            src_ref=src,
            dst_ref=wf.at[w, owner, pl.ds(lo, CUT)],
            send_sem=w_send.at[number],
            recv_sem=w_recv.at[number],
            device_id={"replica": peer},
            device_id_type=MESH,
        )

    def weights_start(*numbers):
        for number in numbers:
            weight_copy(number).start()

    def weights_wait(*numbers):
        for number in numbers:
            weight_copy(number).wait_recv()


    pl.semaphore_wait(barrier, EXPERTS + 3)
    weights_start(0, 6, 1, 7, 2, 3, 4, 5)
    for copy in saved + own_weights + [res_copy]:
        copy.start()

    ids = ids_ref[...].astype(F32)
    expert_row = lax.broadcasted_iota(jnp.int32, (EXPERTS, TOKENS), 0).astype(F32)
    named = jnp.zeros((EXPERTS, TOKENS), F32)
    for k in range(TOP):
        named = named + jnp.where(ids[k : k + 1, :] == expert_row, 1.0, 0.0)
    before = jnp.where(
        lax.broadcasted_iota(jnp.int32, (TOKENS, TOKENS), 0)
        < lax.broadcasted_iota(jnp.int32, (TOKENS, TOKENS), 1),
        1.0,
        0.0,
    ).astype(BF16)
    earlier = dot(named.astype(BF16), before)
    for k in range(TOP):
        id_k = ids[k : k + 1, :]
        slot_k = jnp.sum(jnp.where(id_k == expert_row, earlier, 0.0), axis=0, keepdims=True)
        info[0, k : k + 1, :] = id_k * 32.0 + slot_k
    info[0, TOP : 2 * TOP, :] = gates_ref[...]

    def ring_copy(way, r):
        chain = ((0, 1, 3, 5, 7), (0, 2, 4, 6, 7))[way]
        hop, lo = r // 2, (r % 2 if way == 0 else 1 - r % 2) * 64
        return pltpu.make_async_remote_copy(
            src_ref=grad.at[chain[hop], pl.ds(lo, 64)],
            dst_ref=grad.at[chain[hop + 1], pl.ds(lo, 64)],
            send_sem=g_send.at[way * 7 + r],
            recv_sem=g_recv.at[way * 7 + r],
            device_id={"expert": place(x, z + 1 - 2 * way)},
            device_id_type=MESH,
        )

    def ring_step(r):
        for way in range(2):
            ring_copy(way, r).wait_recv()
            if r + 2 <= 6:
                ring_copy(way, r + 2).start()

    def info_copy(k):
        return pltpu.make_async_remote_copy(
            src_ref=info.at[0],
            dst_ref=info.at[k],
            send_sem=i_send.at[k],
            recv_sem=i_recv.at[k],
            device_id={"expert": place(x, z - turn(k))},
            device_id_type=MESH,
        )

    for k in range(1, RING):
        info_copy(k).start()
    grad_copy.wait()
    for r in range(2):
        for way in range(2):
            ring_copy(way, r).start()

    def dispatch(s):
        return pltpu.make_async_remote_copy(
            src_ref=out.at[s],
            dst_ref=rcv.at[core, s],
            send_sem=a_send.at[s],
            recv_sem=a_recv.at[s],
            device_id={"expert": place(x + lax.rem(s, 4), z)},
            device_id_type=MESH,
        )

    def share(k):
        block = rcv.at[core, pl.ds(4 * k, 4)]
        return pltpu.make_async_remote_copy(
            src_ref=block,
            dst_ref=block,
            send_sem=f_send.at[k],
            recv_sem=f_recv.at[k],
            device_id={"tensor": other},
            device_id_type=MESH,
        )

    def pass_on(g):
        for k in (2 * g, 2 * g + 1):
            for j in range(1, 4):
                dispatch(4 * k + j).wait_recv()
            share(k).start()

    def send_block(k):
        if k > 0:
            info_copy(k).wait_recv()
        row = lax.broadcasted_iota(jnp.int32, (64, 1), 0)
        in_row = jnp.bitwise_and(row, 15)
        base = (jnp.bitwise_and(x + jnp.right_shift(row, 4), 3) * RING + z) * 32
        key_a = (base + in_row).astype(F32)
        key_b = (base + 16 + jnp.bitwise_and(row, 7)).astype(F32)
        hot = weigh = hot_b = weigh_b = jnp.zeros((64, TOKENS), F32)
        for p in range(TOP):
            same = key_a == info[k, p : p + 1, :]
            same_b = key_b == info[k, p : p + 1, :]
            gate = info[k, TOP + p : TOP + p + 1, :]
            hot = hot + jnp.where(same, 1.0, 0.0)
            weigh = weigh + jnp.where(same, gate, 0.0)
            hot_b = hot_b + jnp.where(same_b, 1.0, 0.0)
            weigh_b = weigh_b + jnp.where(same_b, gate, 0.0)
        gate_a = jnp.sum(weigh, axis=1, keepdims=True)
        gate_b = jnp.sum(weigh_b, axis=1, keepdims=True)
        low = jnp.concatenate([hot, jnp.where(in_row < 8, hot_b, 0.0)], axis=0).astype(BF16)
        high = jnp.concatenate([hot, jnp.where(in_row < 8, 0.0, hot_b)], axis=0).astype(BF16)
        left = dot(low, grad[k, :, 0:SHARD])
        right = dot(high, grad[k, :, SHARD:HALF_D])
        rows = (
            (left[0:64] * gate_a, 0),
            (right[0:64] * gate_a, SHARD),
            ((left[64:128] + right[64:128]) * gate_b, HALF_D),
        )
        for value, at in rows:
            value = value.astype(BF16).reshape(4, 16, SHARD)
            rcv[core, 4 * k, :, at : at + SHARD] = value[0]
            out[4 * k + 1 : 4 * k + 4, :, at : at + SHARD] = value[1:4]
        for j in range(1, 4):
            dispatch(4 * k + j).start()

    send_block(0)

    for copy in saved:
        copy.wait()

    def activate(j, _):
        a, u = [], []
        for s in (2 * j, 2 * j + 1):
            block = source(s)
            a.append(gate_pre[block].astype(F32))
            u.append(up_pre[block].astype(F32))
        first = lax.div(j, 4) * TILE
        step = lax.rem(j, 4)
        for lo, hi, at in ((0, 16, first + step * 32), (16, 24, first + 128 + step * 16)):
            a_part = jnp.concatenate([v[lo:hi] for v in a], axis=0)
            u_part = jnp.concatenate([v[lo:hi] for v in u], axis=0)
            sigma = 1.0 / (1.0 + jnp.exp(-a_part))
            silu = a_part * sigma
            to = pl.ds(pl.multiple_of(at, 16), 2 * (hi - lo))
            hid[to, :] = (silu * u_part).astype(BF16)
            fac_up[to, :] = silu
            fac_gate[to, :] = u_part * sigma * (1.0 + a_part * (1.0 - sigma))
        return 0

    lax.fori_loop(0, EXPERTS // 2, activate, 0)

    def tile_of(g):
        return pl.ds(pl.multiple_of(g * TILE, TILE), TILE)

    def unfold(g):
        for k in (2 * g, 2 * g + 1):
            share(k).wait()
        for h in range(2):
            routed[h, g * TILE : g * TILE + 128, :] = rcv[h, g * 8 : g * 8 + 8, :, 0:HALF_D].reshape(128, HALF_D)
            raw = rcv[h, g * 8 : g * 8 + 8, :, HALF_D:WIDE].astype(F32).reshape(8, 2, 8, SHARD)
            for q in range(2):
                routed[h, g * TILE + 128 : (g + 1) * TILE, q * SHARD : (q + 1) * SHARD] = (
                    raw[:, q].reshape(64, SHARD).astype(BF16)
                )

    def w_half(w, h):
        return wf[w, pl.ds(2 * h, 2)].reshape(HALF_D, GROUP)

    def hidden_grads(g, _):
        rows = tile_of(g)
        total = dot(routed[0, rows, :], w_half(0, 0)) + dot(routed[1, rows, :], w_half(0, 1))
        by_gate = (total * fac_gate[rows, :]).astype(BF16)
        by_up = (total * fac_up[rows, :]).astype(BF16)
        for lo, hi, to in ((0, 128, g * 128), (128, TILE, ROWS_A + g * 64)):
            to = pl.ds(pl.multiple_of(to, 64), hi - lo)
            gate_grad[to, :] = by_gate[lo:hi]
            up_grad[to, :] = by_up[lo:hi]
        return 0

    def correct(lo, hi, first, last, halves):
        for h in halves:
            def step(t, _, h=h):
                columns = pl.ds(pl.multiple_of(t * 256, 256), 256)
                rows = pl.ds(pl.multiple_of(h * HALF_D + t * 256, 256), 256)
                total = dot(routed[h, lo:hi, columns], hid[lo:hi, :], ((0,), (0,)))
                total = total + (res[rows, :].astype(F32) if first else corr[rows, :])
                corr[rows, :] = total
                if last:
                    for b in range(2):
                        top = jnp.max(jnp.abs(total[b * BLOCK : (b + 1) * BLOCK]), axis=0, keepdims=True)
                        own_max[pl.ds(h * 14 + t * 2 + b, 1), :] = top
                return 0

            lax.fori_loop(0, 7, step, 0)

    SPANS = ((0, SHARD), (SHARD, WIDE))

    def half_of(stage):
        return near if stage == 0 else 1 - near

    def swap(stage, phase, g):
        lo, hi = SPANS[phase]
        block = (pl.ds(g * 8, 8), slice(None), slice(lo, hi))
        return pltpu.make_async_remote_copy(
            src_ref=part.at[(stage,) + block],
            dst_ref=part_got.at[block],
            send_sem=p_send.at[phase * 4 + g],
            recv_sem=p_recv.at[phase * 4 + g],
            device_id={"tensor": other},
            device_id_type=MESH,
        )

    def partial(stage, phase):
        shards = ((y, pair), (next_, opposite))[stage]

        for lo in range(0, SHARD, 256):
            hi = min(lo + 256, SHARD)

            def value(rows, s, lo=lo, hi=hi):
                return dot(gate_grad[rows, :], wf[1, s, lo:hi, :], ((1,), (1,))) + dot(
                    up_grad[rows, :], wf[2, s, lo:hi, :], ((1,), (1,))
                )

            at = phase * SHARD + lo
            part[stage, :, :, at : at + hi - lo] = (
                value(slice(0, ROWS_A), shards[phase]).astype(BF16).reshape(EXPERTS, 16, hi - lo)
            )
            if phase == 1:
                both = [value(slice(ROWS_A, SLOTS), s).reshape(EXPERTS, 1, 8, hi - lo) for s in shards]
                both = jnp.concatenate(both, axis=1).reshape(EXPERTS, 16, hi - lo)
                part[stage, :, :, HALF_D + lo : HALF_D + hi] = both.astype(BF16)

        @pl.when(half_of(stage) != core)
        def _():
            for g in range(4):
                swap(stage, phase, g).start()

    def give_back(phase, s):
        lo, hi = SPANS[phase]
        return pltpu.make_async_remote_copy(
            src_ref=out.at[s, :, lo:hi],
            dst_ref=ret.at[s, :, lo:hi],
            send_sem=r_send.at[phase * EXPERTS + s],
            recv_sem=r_recv.at[phase * EXPERTS + s],
            device_id={"expert": source(s)},
            device_id_type=MESH,
        )

    def send_back(stage, phase):
        lo, hi = SPANS[phase]

        def summed(s):
            return (part[stage, s, :, lo:hi].astype(F32) + part_got[s, :, lo:hi].astype(F32)).astype(BF16)

        def one(s, _):
            out[s, :, lo:hi] = summed(s)
            give_back(phase, s).start()
            return 0

        @pl.when(half_of(stage) == core)
        def _():
            for g in range(4):
                swap(stage, phase, g).wait_recv()
                if g == 0:
                    ret[0, :, lo:hi] = summed(0)
                lax.fori_loop(max(1, g * 8), g * 8 + 8, one, 0)

    ring_step(0)
    ring_step(1)
    weights_wait(0)
    weights_start(12)
    send_block(1)
    send_block(2)
    ring_step(2)
    ring_step(3)
    weights_wait(1)
    weights_start(13, 8, 9)
    send_block(3)
    send_block(4)
    pass_on(0)
    ring_step(4)
    unfold(0)
    ring_step(5)
    send_block(5)
    send_block(6)
    pass_on(1)
    unfold(1)
    res_copy.wait()
    correct(0, 2 * TILE, True, False, (0,))
    ring_step(6)
    send_block(7)
    pass_on(2)
    unfold(2)
    pass_on(3)
    correct(0, 2 * TILE, True, False, (1,))
    unfold(3)
    own_weights[0].wait()
    weights_wait(6, 7, 12, 13)
    lax.fori_loop(0, 4, hidden_grads, 0)
    own_weights[1].wait()
    own_weights[2].wait()
    partial(0, 0)
    weights_start(11)

    def dispatched(i, _):
        dispatch(lax.div(i, 3) * 4 + 1 + lax.rem(i, 3)).wait_send()
        return 0

    lax.fori_loop(0, 24, dispatched, 0)
    send_back(0, 0)
    weights_wait(8, 4)
    weights_start(15)
    correct(2 * TILE, SLOTS, False, True, (0, 1))
    for number in (12, 13):
        weight_copy(number).wait_send()

    own_max[D // BLOCK :, :] = jnp.zeros((32 - D // BLOCK, GROUP), F32)
    maxima[y] = own_max[...].astype(BF16)

    def max_copy(i):
        return pltpu.make_async_remote_copy(
            src_ref=maxima.at[y],
            dst_ref=maxima.at[y],
            send_sem=m_send.at[i],
            recv_sem=m_recv.at[i],
            device_id={"replica": (opposite, pair, next_)[i]},
            device_id_type=MESH,
        )

    for i in range(3):
        max_copy(i).start()
    weights_start(10, 14)
    weights_wait(2, 3, 5)
    weights_wait(9)
    weights_start(16)
    partial(0, 1)
    send_back(0, 1)

    row = lax.broadcasted_iota(jnp.int32, (ROWS_A, 1), 0)
    in_row = jnp.bitwise_and(row, 15)
    ring = jnp.right_shift(row, 6)
    turned = jnp.right_shift(ring + 1, 1) * (1 - 2 * jnp.bitwise_and(ring, 1))
    expert = jnp.bitwise_and(x + jnp.right_shift(row, 4), 3) * RING + jnp.bitwise_and(z - turned, RING - 1)
    key_a = (expert * 32 + in_row).astype(F32)
    key_b = (expert * 32 + 16 + jnp.bitwise_and(row, 7)).astype(F32)
    hot = hot_b = jnp.zeros((ROWS_A, TOKENS), F32)
    for p in range(TOP):
        hot = hot + jnp.where(key_a == info[0, p : p + 1, :], 1.0, 0.0)
        hot_b = hot_b + jnp.where(key_b == info[0, p : p + 1, :], 1.0, 0.0)
    pick[0] = hot
    pick[1] = jnp.where(in_row < 8, hot_b, 0.0)
    pick[2] = jnp.where(in_row < 8, 0.0, hot_b)
    for j in range(3):
        pick_t[j] = jnp.transpose(pick[j]).astype(BF16)

    weights_wait(11)
    weights_start(17)
    for i in range(3):
        max_copy(i).wait()
    largest = maxima[0].astype(F32)
    for r in range(1, REPLICAS):
        largest = jnp.maximum(largest, maxima[r].astype(F32))
    scales_ref[...] = largest[0 : D // BLOCK] + 1e-6
    results = [pltpu.make_async_copy(scales_ref, scales_hbm, l_sem.at[7])]
    results[0].start()

    def code(b, _):
        rows = pl.ds(pl.multiple_of(b * BLOCK, BLOCK), BLOCK)
        res[rows, :] = (corr[rows, :] / scales_ref[pl.ds(b, 1), :]).astype(BF16)
        return 0

    lax.fori_loop(0, D // BLOCK, code, 0)

    PART = CUT // 2

    def code_rows(owner, lo, n):
        return pl.ds(pl.multiple_of(owner * SHARD + lo, PART), n)

    def code_got(i):
        if i < 4:
            return wf.at[0, i // 2, pl.ds(i % 2 * CUT, CUT)]
        return wf.at[0, 2, pl.ds(i % 2 * CUT + i // 6 * PART, PART)]

    def code_copy(i):
        if i < 4:
            owner = (opposite, opposite, pair, next_)[i]
            src = res.at[code_rows(owner, (CUT, 0, CUT, 0)[i], CUT)]
        else:
            src = code_sum.at[i % 2, pl.ds(i // 6 * PART, PART)]
        return pltpu.make_async_remote_copy(
            src_ref=src,
            dst_ref=code_got(i),
            send_sem=c_send.at[i],
            recv_sem=c_recv.at[i],
            device_id={"replica": (pair, next_)[i % 2]},
            device_id_type=MESH,
        )

    for i in range(4):
        code_copy(i).start()

    def code_pass(i):
        code_copy(1 - i).wait_recv()
        owner, lo = ((pair, 0), (next_, CUT))[i]
        own_codes = res[code_rows(owner, lo, CUT), :].astype(F32)
        code_sum[i] = (own_codes + code_got(1 - i)[...].astype(F32)).astype(BF16)
        code_copy(4 + i).start()
        code_copy(6 + i).start()

    weights_wait(10)
    partial(1, 0)
    send_back(1, 0)
    weights_wait(14, 15, 16, 17)
    partial(1, 1)
    send_back(1, 1)
    for i in range(2):
        code_pass(i)

    def came_back(s, _):
        give_back(0, s).wait()
        give_back(1, s).wait()
        return 0

    def combine(g):
        rows = slice(g * 128, (g + 1) * 128)
        back_b = ret[g * 8 : g * 8 + 8, :, HALF_D:WIDE].reshape(128, SHARD)
        for q in range(2):
            columns = slice(q * SHARD, (q + 1) * SHARD)
            total = dot(pick_t[0, :, rows], ret[g * 8 : g * 8 + 8, :, columns].reshape(128, SHARD))
            total = total + dot(pick_t[1 + q, :, rows], back_b)
            if g > 0:
                total = total + total_in[:, columns]
            if g < 3:
                total_in[:, columns] = total
            else:
                shard = jnp.where(core == near, (y, pair)[q], (next_, opposite)[q])
                to = pl.ds(pl.multiple_of(lax.rem(shard, 2) * SHARD, SHARD), SHARD)
                grad_in_ref[:, to] = total.astype(BF16)

    for g in range(3):
        lax.fori_loop(max(1, g * 8), g * 8 + 8, came_back, 0)
        combine(g)

    lax.fori_loop(24, EXPERTS, came_back, 0)
    combine(3)
    results.append(pltpu.make_async_copy(grad_in_ref, grad_in_hbm, l_sem.at[8]))
    results[1].start()

    code_copy(2).wait_recv()
    code_copy(3).wait_recv()
    for at, first, second in ((0, 3, 4), (2, 2, 5), (1, 3, 6), (3, 2, 7)):
        code_copy(second).wait_recv()
        lo = at * PART

        def add_codes(t, _, lo=lo, first=first):
            rows = pl.ds(pl.multiple_of(lo + t * 32, 32), 32)
            total = res[pl.ds(pl.multiple_of(y * SHARD + lo + t * 32, 32), 32), :].astype(F32)
            part_of = lo % CUT + t * 32
            total = total + wf[0, 1, pl.ds(pl.multiple_of(first % 2 * CUT + part_of, 32), 32), :].astype(F32)
            total = total + wf[0, 2, pl.ds(pl.multiple_of((1 - first % 2) * CUT + part_of, 32), 32), :].astype(F32)
            sums_ref[rows, :] = total
            return 0

        lax.fori_loop(0, PART // 32, add_codes, 0)
        rows = pl.ds(lo, PART)
        results.append(pltpu.make_async_copy(sums_ref.at[rows], sums_hbm.at[rows], l_sem.at[9 + at]))
        results[-1].start()

    for number in range(18):
        if number not in (12, 13):
            weight_copy(number).wait_send()
    for k in range(1, RING):
        info_copy(k).wait_send()
    for r in range(7):
        for way in range(2):
            ring_copy(way, r).wait_send()
    for i in range(8):
        code_copy(i).wait_send()
    for stage, half in ((0, near), (1, 1 - near)):
        @pl.when(half != core)
        def _(stage=stage):
            for g in range(4):
                for phase in range(2):
                    swap(stage, phase, g).wait_send()
    for copy in results:
        copy.wait()


def hand_out(grad_ref, sums_ref, scales_ref, grad_out, sums_out, scales_out, grad, sums, scales, flat, come, go):
    half = SHARD // 2
    pieces = [(scales_ref, scales, flat, scales_out), (grad_ref, grad, grad, grad_out)]
    for t in range(2):
        rows = pl.ds(t * half, half)
        pieces.append((sums_ref.at[rows], sums.at[rows], sums.at[rows], sums_out.at[rows]))
    into = [pltpu.make_async_copy(p[0], p[1], come.at[i]) for i, p in enumerate(pieces)]
    away = [pltpu.make_async_copy(p[2], p[3], go.at[i]) for i, p in enumerate(pieces)]
    for copy in into:
        copy.start()
    into[0].wait()
    for b in range(D // BLOCK):
        flat[b] = scales[b : b + 1, :]
    away[0].start()
    for first, second in zip(into[1:], away[1:]):
        first.wait()
        second.start()
    for copy in away:
        copy.wait()


def local(grad_out, gates, expert_ids, gate_pre, up_pre, w_gate, w_up, w_down, residual):
    whole = pl.BlockSpec(memory_space=pltpu.VMEM)
    hbm = pl.BlockSpec(memory_space=pl.ANY)
    message = (EXPERTS, 16, WIDE)
    dma = pltpu.SemaphoreType.DMA
    saved = [a.reshape(EXPERTS, CAP, GROUP) for a in (gate_pre, up_pre)]
    grad_in, code_sums, scales = pl.pallas_call(
        kernel,
        out_shape=(
            jax.ShapeDtypeStruct((TOKENS, HALF_D), BF16),
            jax.ShapeDtypeStruct((SHARD, GROUP), F32),
            jax.ShapeDtypeStruct((D // BLOCK, GROUP), F32),
        ),
        in_specs=[whole, whole] + [hbm] * 7,
        out_specs=(hbm, hbm, hbm),
        scratch_shapes=[
            pltpu.VMEM((TOKENS, HALF_D), BF16),
            pltpu.VMEM((SHARD, GROUP), F32),
            pltpu.VMEM((D // BLOCK, GROUP), F32),
            pltpu.VMEM(message, BF16),
            pltpu.VMEM((2,) + message, BF16),
            pltpu.VMEM(message, BF16),
            pltpu.VMEM((2,) + message, BF16),
            pltpu.VMEM(message, BF16),
            pltpu.VMEM((3, REPLICAS, SHARD, GROUP), BF16),
            pltpu.VMEM((2, SLOTS, HALF_D), BF16),
            pltpu.VMEM((3, ROWS_A, TOKENS), F32),
            pltpu.VMEM((3, TOKENS, ROWS_A), BF16),
            pltpu.VMEM((RING, 2 * TOP, TOKENS), F32),
            pltpu.VMEM((RING, TOKENS, HALF_D), BF16),
            pltpu.VMEM((EXPERTS, CAP, GROUP), BF16),
            pltpu.VMEM((EXPERTS, CAP, GROUP), BF16),
            pltpu.VMEM((SLOTS, GROUP), BF16),
            pltpu.VMEM((SLOTS, GROUP), F32),
            pltpu.VMEM((SLOTS, GROUP), F32),
            pltpu.VMEM((SLOTS, GROUP), BF16),
            pltpu.VMEM((SLOTS, GROUP), BF16),
            pltpu.VMEM((D, GROUP), BF16),
            pltpu.VMEM((D, GROUP), F32),
            pltpu.VMEM((2, CUT, GROUP), BF16),
            pltpu.VMEM((32, GROUP), F32),
            pltpu.VMEM((REPLICAS, 32, GROUP), BF16),
            pltpu.VMEM((TOKENS, HALF_D), F32),
            dma((14,)),
            dma((14,)),
            dma((RING,)),
            dma((RING,)),
            dma((EXPERTS,)),
            dma((EXPERTS,)),
            dma((EXPERTS,)),
            dma((EXPERTS,)),
            dma((2 * EXPERTS,)),
            dma((2 * EXPERTS,)),
            dma((18,)),
            dma((18,)),
            dma((8,)),
            dma((8,)),
            dma((3,)),
            dma((3,)),
            dma((8,)),
            dma((8,)),
            dma((13,)),
        ],
        compiler_params=pltpu.CompilerParams(
            collective_id=0, has_side_effects=True, vmem_limit_bytes=62 * 2**20
        ),
        cost_estimate=pl.CostEstimate(flops=11_300_000_000, bytes_accessed=14_000_000, transcendentals=400_000),
    )(
        expert_ids.T, gates.T, grad_out, *saved, w_gate[0], w_up[0], w_down[0], residual[0]
    )
    grad_in, code_sums, scales = pl.pallas_call(
        hand_out,
        out_shape=(
            jax.ShapeDtypeStruct((TOKENS, HALF_D), BF16),
            jax.ShapeDtypeStruct((SHARD, GROUP), F32),
            jax.ShapeDtypeStruct((D // BLOCK, 1, GROUP), F32),
        ),
        in_specs=[hbm, hbm, hbm],
        out_specs=(hbm, hbm, hbm),
        scratch_shapes=[
            pltpu.VMEM((TOKENS, HALF_D), BF16),
            pltpu.VMEM((SHARD, GROUP), F32),
            pltpu.VMEM((D // BLOCK, GROUP), F32),
            pltpu.VMEM((D // BLOCK, 1, GROUP), F32),
            dma((4,)),
            dma((4,)),
        ],
        compiler_params=pltpu.CompilerParams(vmem_limit_bytes=60 * 2**20),
    )(grad_in, code_sums, scales)
    return grad_in, code_sums[None], scales.reshape(1, D // BLOCK, GROUP)


def solution(mesh):
    spec = P("expert", "replica", "tensor")
    tokens = P(("expert", "replica"), None)
    in_specs = (tokens,) * 3 + (spec,) * 6
    out_specs = (P(("expert", "replica"), "tensor"), spec, P("expert", None, "tensor"))
    return jax.shard_map(local, mesh=mesh, in_specs=in_specs, out_specs=out_specs, check_vma=False)
```
